128 devices in a mesh: gx: 8 (over z, core), gy: 16 (over y, x).
Axes of the slice: x: 4, y: 4, z: 4, core: 2. Of those that a mesh axis runs over, the one named last changes fastest.
Arguments:
- tokens: bfloat16 [2, 512, 18432], P(None, 'gy', 'gx'), may hold values from -250 to 250
- norm_gain: float32 [18432], P('gx'), may hold values from 0.25 to 1.75
- w_query: bfloat16 [18432, 12288], P('gx', 'gy'), may hold values from -0.046875 to 0.046875
- w_kv: bfloat16 [18432, 512], P('gx'), may hold values from -0.046875 to 0.046875
- w_out: bfloat16 [12288, 18432], P('gy', 'gx'), may hold values from -0.0546875 to 0.0546875
- cache_keys: bfloat16 [512, 2048, 256], P(('gx', 'gy')), may hold values from -1000 to 1000
- cache_values: bfloat16 [512, 2048, 256], P(('gx', 'gy')), may hold values from -6 to 6
- lengths: int32 [512], P(('gx', 'gy')), may hold values from 1024 to 2048, as said below
Outputs:
- attn_branch: bfloat16 [2, 512, 18432], P(None, 'gy', 'gx')
The draws below stay inside these ranges and needn't reach their ends.
Inputs may be any that keep to these rules, and one draw needn't show every extreme that they name: `lengths`: each row's valid cache length; some row holds exactly 2048 and some exactly 1024.
All inputs are finite; a program needn't handle non-finite values.
Results may differ from the reference program's by a relative error of at most 0.02.
The reference program's roundings to bfloat16 on the way count: a program that leaves them out, or rounds other values in their place, can miss the bound.
Values may be sent and summed in bfloat16 or wider, within the bound.
No kernel may reach another device: no remote copies, remote signals or barrier semaphores. Data moves between devices by JAX's collectives and lax.ppermute only.
A program may use at most 128 MiB of HBM per device.

```python
import math
import jax
import jax.numpy as jnp
from jax import lax

D = 18432
HEADS = 48
HEAD_DIM = 256
CACHE = 2048
BATCH = 512
N_GY = 16


def draw_tokens(key, part):
    key = jax.random.fold_in(key, 11)
    key_base, key_rows = jax.random.split(key, 2)
    row_scale = jnp.exp(jax.random.uniform(key_rows, (2, BATCH, 1), jnp.float32, 0.0, math.log(10.0)))
    base_vals = jnp.clip(jax.random.normal(key_base, (2, BATCH, D), jnp.float32), -6.0, 6.0)
    growth = math.log(3.0)
    column_scale = jnp.exp(growth * jnp.arange(D, dtype=jnp.float32) / (D - 1))
    return (base_vals * row_scale * column_scale[None, None, :]).astype(jnp.bfloat16)


def draw_cache_keys(key, part):
    key = jax.random.fold_in(key, 23)
    key_base = jax.random.fold_in(key, 0)
    base_vals = jnp.clip(jax.random.normal(key_base, (BATCH, CACHE, HEAD_DIM), jnp.float32), -6.0, 6.0)
    keys_out = base_vals
    return keys_out.astype(jnp.bfloat16)


def draw_lengths(key, part):
    key = jax.random.fold_in(key, 37)
    key_lens, key_first, key_offset = jax.random.split(key, 3)
    lens_out = jax.random.randint(key_lens, (BATCH,), CACHE // 2, CACHE + 1)
    first_row = jax.random.randint(key_first, (), 0, BATCH)
    other_row = (first_row + 1 + jax.random.randint(key_offset, (), 0, BATCH - 1)) % BATCH
    lens_out = lens_out.at[first_row].set(CACHE)
    lens_out = lens_out.at[other_row].set(CACHE // 2)
    return lens_out.astype(jnp.int32)


def levels(key, dims, shards, least, high):
    level = 1.0
    for axis_at, shards_of in shards:
        draws = jax.random.uniform(jax.random.fold_in(jax.random.fold_in(key, 6), axis_at), (shards_of,), jnp.float32, least / len(shards), high / len(shards))
        level = level * jnp.repeat(jnp.exp(draws), dims[axis_at] // shards_of).reshape((-1,) + (1,) * (len(dims) - 1 - axis_at))
    return level


def bell_draw(rng, extent, scale, limit, pieces=(), held_as=jnp.bfloat16):
    entries = jax.random.normal(rng, extent, jnp.float32) * scale
    if len(pieces) > 0:
        entries = levels(rng, extent, pieces, -0.22, 0.18) * entries
    return jnp.clip(entries, min=-limit, max=limit).astype(held_as)


def setup_inputs(seed: int = 0) -> dict:
    key_of = jax.random.split(jax.random.key(seed), 9)
    return {
        "tokens": draw_tokens(jax.random.fold_in(key_of[8], 71), 0),
        "norm_gain": jnp.clip(1.0 + 0.15 * jax.random.normal(key_of[1], (D,), jnp.float32), 0.25, 1.75),
        "w_query": bell_draw(key_of[2], (D, HEADS * HEAD_DIM), D ** -0.5, 0.046875, ((0, 8), (1, 16))),
        "w_kv": bell_draw(key_of[3], (D, 2 * HEAD_DIM), D ** -0.5, 0.046875, ((0, 8),)),
        "w_out": bell_draw(key_of[4], (HEADS * HEAD_DIM, D), (HEADS * HEAD_DIM) ** -0.5, 0.0546875, ((0, 16), (1, 8))),
        "cache_keys": draw_cache_keys(jax.random.fold_in(key_of[8], 71), 0),
        "cache_values": bell_draw(key_of[6], (BATCH, CACHE, HEAD_DIM), 1.0, 6.0, ((0, 128),)),
        "lengths": draw_lengths(jax.random.fold_in(key_of[8], 71), 0),
    }


def layer_norm(inputs, gain_vec):
    values_f = inputs.astype(jnp.float32)
    average = lax.optimization_barrier(jnp.mean(values_f, axis=-1, keepdims=True))
    centred = values_f - average
    spread = lax.optimization_barrier(jnp.mean(centred * centred, axis=-1, keepdims=True))
    return (centred * lax.rsqrt(spread + 1e-05) * gain_vec.astype(jnp.float32)).astype(jnp.bfloat16)

def attend(query, keys_all, values_all, lens_here, new_keys, new_values):
    factor = query.shape[-1] ** (-0.5)
    query_f = query.astype(jnp.float32)
    scores_c = jnp.einsum('rhd,rld->rhl', query_f, keys_all.astype(jnp.float32)) * factor
    position = jnp.arange(keys_all.shape[1], dtype=jnp.int32)
    usable = position[None, None, :] < lens_here.astype(jnp.int32)[:, None, None]
    scores_c = jnp.where(usable, scores_c, -1e+30)
    scores_n = jnp.einsum('rhd,rsd->rhs', query_f, new_keys.astype(jnp.float32)) * factor
    highest = jnp.maximum(lax.optimization_barrier(jnp.max(scores_c, axis=-1)), lax.optimization_barrier(jnp.max(scores_n, axis=-1)))[..., None]
    exp_c = jnp.exp(scores_c - highest)
    exp_n = jnp.exp(scores_n - highest)
    totals = lax.optimization_barrier(jnp.sum(exp_c, axis=-1, keepdims=True)) + lax.optimization_barrier(jnp.sum(exp_n, axis=-1, keepdims=True))
    weight_c = (exp_c / totals).astype(jnp.bfloat16)
    weight_n = (exp_n / totals).astype(jnp.bfloat16)
    result = jnp.einsum('rhl,rld->rhd', weight_c.astype(jnp.float32), values_all.astype(jnp.float32))
    result = result + jnp.einsum('rhs,rsd->rhd', weight_n.astype(jnp.float32), new_values.astype(jnp.float32))
    return result.reshape(result.shape[0], -1).astype(jnp.bfloat16)

def grouped_output(mixed, w_out):
    cols = HEADS * HEAD_DIM // N_GY

    def add_group(index, total):
        start = (index * cols).astype(jnp.int32)
        left = lax.dynamic_slice_in_dim(mixed, start, cols, 1)
        right = lax.dynamic_slice_in_dim(w_out, start, cols, 0)
        partial_value = jnp.dot(left, right, preferred_element_type=jnp.float32).astype(jnp.bfloat16)
        return total + partial_value.astype(jnp.float32)
    start_total = jnp.zeros((mixed.shape[0], w_out.shape[1]), jnp.float32)
    return lax.fori_loop(0, N_GY, add_group, start_total).astype(jnp.bfloat16)

def reference(tokens, norm_gain, w_query, w_kv, w_out, cache_keys, cache_values, lengths):
    block_rows = math.gcd(BATCH, 64)
    blocks = BATCH // block_rows
    results = []
    kept_keys = []
    kept_values = []
    for section in range(2):
        normed = layer_norm(tokens[section], norm_gain)
        query = jnp.dot(normed, w_query, preferred_element_type=jnp.float32).astype(jnp.bfloat16)
        key_value = jnp.dot(normed, w_kv, preferred_element_type=jnp.float32).astype(jnp.bfloat16)
        kept_keys.append(key_value[:, :HEAD_DIM])
        kept_values.append(key_value[:, HEAD_DIM:])
        new_keys = jnp.stack(kept_keys, axis=1)
        new_values = jnp.stack(kept_values, axis=1)
        heads_view = query.reshape(blocks, block_rows, HEADS, HEAD_DIM)

        def one_block(packed):
            return attend(*packed)
        mixed = lax.map(one_block, (heads_view, cache_keys.reshape(blocks, block_rows, CACHE, HEAD_DIM), cache_values.reshape(blocks, block_rows, CACHE, HEAD_DIM), lengths.reshape(blocks, block_rows), new_keys.reshape(blocks, block_rows, section + 1, HEAD_DIM), new_values.reshape(blocks, block_rows, section + 1, HEAD_DIM)))
        mixed = mixed.reshape(BATCH, HEADS * HEAD_DIM)
        results.append(grouped_output(mixed, w_out))
    return jnp.stack(results, axis=0)
```

```python
import jax
import jax.numpy as jnp
from jax import lax
from jax.experimental import pallas as pl
from jax.experimental.pallas import tpu as pltpu
from jax.sharding import PartitionSpec as P

HEADS = 48
BF = jnp.bfloat16
F32 = jnp.float32
VMEM_LIMIT = 48 * 1024 * 1024


def flat_perm(place):
    pairs = []
    for gx in range(8):
        for gy in range(16):
            z, c, y, x = gx // 2, gx % 2, gy // 4, gy % 4
            z2, c2, y2, x2 = place(z, c, y, x)
            pairs.append((gx * 16 + gy, ((z2 % 4) * 2 + c2) * 16 + (y2 % 4) * 4 + x2 % 4))
    return pairs


def send(value, place):
    return lax.ppermute(value, ("gx", "gy"), flat_perm(place))


def along_x(z, c, y, x, d):
    return (z, c, y, x + d)


def along_y(z, c, y, x, d):
    return (z, c, y + d, x)


def first_axis(d):
    return lambda z, c, y, x: (z, c, y, x + d) if c == 0 else (z, c, y + d, x)


def second_axis(d):
    return lambda z, c, y, x: (z, c, y + d, x) if c == 0 else (z, c, y, x + d)


def z_axis(d):
    return lambda z, c, y, x: (z + d, c, y, x)


def other_core(z, c, y, x):
    return (z, 1 - c, y, x)


def whole(shape):
    return pl.BlockSpec(shape, lambda *_: (0,) * len(shape))


def kernel_call(body, grid, in_specs, out_specs, out_shape, scratch, flops, nbytes, name):
    return pl.pallas_call(
        body,
        grid_spec=pltpu.PrefetchScalarGridSpec(
            num_scalar_prefetch=1,
            grid=grid,
            in_specs=in_specs,
            out_specs=out_specs,
            scratch_shapes=scratch,
        ),
        out_shape=out_shape,
        compiler_params=pltpu.CompilerParams(vmem_limit_bytes=VMEM_LIMIT),
        cost_estimate=pl.CostEstimate(flops=flops, bytes_accessed=nbytes, transcendentals=0),
        name=name,
    )


def one_hot(rows, cols, source):
    row = lax.broadcasted_iota(jnp.int32, (rows, cols), 0)
    col = lax.broadcasted_iota(jnp.int32, (rows, cols), 1)
    return jnp.where(col == source(row), 1.0, 0.0).astype(BF)


def project_body(place, own, plus, minus, half_a, half_b, stat, gain, wq, wkv, out, raw, normed, sems):
    x, y, c, part = place[0], place[1], place[3], place[4]
    width_q = wq.shape[1]
    blocks = [(own, k, 0, k) for k in range(4)]
    blocks += [(plus, k, 1, k) for k in range(4)]
    blocks += [(minus, k, 3, k) for k in range(4)]
    blocks += [(half_a, k, 2, k) for k in range(2)]
    blocks += [(half_b, k, 2, k + 2) for k in range(2)]
    for ref, k, d1, d2 in blocks:
        bx = (x + jnp.where(c == 0, d2, d1)) & 3
        by = (y + jnp.where(c == 0, d1, d2)) & 3

        @pl.when((bx >> 1) == part)
        def _(ref=ref, k=k, bx=bx, by=by):
            slot = by * 2 + (bx & 1)
            pltpu.make_async_copy(ref.at[pl.ds(k * 64, 64)], raw.at[slot], sems.at[slot]).start()

    for slot in range(8):
        pltpu.make_async_copy(own.at[pl.ds(0, 64)], raw.at[slot], sems.at[slot]).wait()
        st = stat[(slot // 2) * 4 + 2 * part + slot % 2]
        value = raw[slot].astype(F32)
        normed[slot] = ((value - st[:, 0:1]) * st[:, 1:2] * gain[...]).astype(BF)
    for m in range(2):
        left = normed[4 * m : 4 * m + 4].reshape(256, normed.shape[-1])
        q = jnp.dot(left, wq[...], preferred_element_type=F32)
        kv = jnp.dot(left, wkv[...], preferred_element_type=F32)
        out[2 * m : 2 * m + 2, :, :width_q] = q.reshape(2, 128, width_q)
        out[2 * m : 2 * m + 2, :, width_q:] = kv.reshape(2, 128, kv.shape[1])


def project(place, pieces, stat, gain, wq, wkv):
    width, nq = wq.shape
    n = nq + wkv.shape[1]
    any_spec = pl.BlockSpec(memory_space=pl.ANY)
    return kernel_call(
        project_body,
        (1,),
        [any_spec] * 5 + [whole(stat.shape), whole(gain.shape), whole(wq.shape), whole(wkv.shape)],
        whole((4, 128, n)),
        jax.ShapeDtypeStruct((4, 128, n), F32),
        [
            pltpu.VMEM((8, 64, width), BF),
            pltpu.VMEM((8, 64, width), BF),
            pltpu.SemaphoreType.DMA((8,)),
        ],
        2 * 512 * width * n,
        512 * width * 2 + width * n * 2 + 512 * n * 4,
        "project",
    )(place, *pieces, stat, gain, wq, wkv)


def pair_sum_body(place, keep, got, own, s1, s2, s3):
    value = keep[0] + got[0]
    step = pl.program_id(0)

    @pl.when(step == 0)
    def _():
        own[...] = value

    for d, ref in ((1, s1), (2, s2), (3, s3)):

        @pl.when(step == d)
        def _(ref=ref):
            ref[...] = value.astype(BF)


def pair_sum(place, keep, got):
    n = keep.shape[-1]
    block = pl.BlockSpec((1, 128, n), lambda d, p: ((p[2] + d) & 3, 0, 0))
    return kernel_call(
        pair_sum_body,
        (4,),
        [block, block],
        [whole((128, n))] * 4,
        [jax.ShapeDtypeStruct((128, n), F32)] + [jax.ShapeDtypeStruct((128, n), BF)] * 3,
        [],
        512 * n,
        2 * 512 * n * 4,
        "pair_sum",
    )(place, keep, got)


def finish_query_body(place, own, r1, r2, r3, out):
    total = own[...] + r1[...].astype(F32) + r2[...].astype(F32) + r3[...].astype(F32)
    order = one_hot(
        128, 128, lambda i: (i & 64) + ((i >> 2) & 1) * 32 + ((i >> 3) & 7) * 4 + (i & 3)
    )
    moved = jnp.dot(order, total.astype(BF), preferred_element_type=F32)
    out[...] = moved.reshape(16, 8, moved.shape[-1]).astype(BF)


def finish_query(place, own, got):
    n = own.shape[-1]
    return kernel_call(
        finish_query_body,
        (1,),
        [whole((128, n))] * 4,
        whole((16, 8, n)),
        jax.ShapeDtypeStruct((16, 8, n), BF),
        [],
        2 * 128 * 128 * n,
        128 * n * 12,
        "finish_query",
    )(place, own, *got)


def attend_body(lens, x, keys, values, out, acc):
    row = pl.program_id(0)
    nq = out.shape[-1]
    dim = keys.shape[-1]
    length = keys.shape[1]
    piece = x.shape[-1] - nq
    factor = dim ** (-0.5)
    flat = x[...].astype(F32).reshape(128, x.shape[-1]).astype(BF)
    pick = one_hot(32, 128, lambda i: (i >> 1) * 8 + (i & 1) * 4 + row)
    mine = jnp.dot(pick, flat[:, :nq], preferred_element_type=F32).astype(BF)
    heads = nq // dim
    query = jnp.concatenate([mine[:, h * dim : (h + 1) * dim] for h in range(heads)], axis=0)
    count = query.shape[0]

    spread = one_hot(piece, 16 * piece, lambda i: i)
    lane = lax.broadcasted_iota(jnp.int32, (piece, 16 * piece), 1)
    sub = lax.broadcasted_iota(jnp.int32, (piece, 16 * piece), 0)
    spread = jnp.where(lane % piece == sub, 1.0, 0.0).astype(BF)
    tiled = jnp.dot(flat[:, nq:], spread, preferred_element_type=F32)
    lane = lax.broadcasted_iota(jnp.int32, (128, 16 * piece), 1)
    sub = lax.broadcasted_iota(jnp.int32, (128, 16 * piece), 0)
    tiled = jnp.where(lane // piece == sub >> 3, tiled, 0.0).astype(BF)
    sub = lax.broadcasted_iota(jnp.int32, (8, 128), 0)
    lane = lax.broadcasted_iota(jnp.int32, (8, 128), 1)
    gather = jnp.where((lane & 7) == sub * 4 + row, 1.0, 0.0).astype(BF)
    fresh = jnp.dot(gather, tiled, preferred_element_type=F32)

    scores = (
        lax.dot_general(query, keys[0], (((1,), (1,)), ((), ())), preferred_element_type=F32)
        * factor
    )
    position = lax.broadcasted_iota(jnp.int32, (count, length), 1)
    scores = jnp.where(position < lens[row], scores, -1e30)
    query_f = query.astype(F32)
    new_0 = jnp.sum(query_f * fresh[0:1, :dim], axis=-1, keepdims=True) * factor
    new_1 = jnp.sum(query_f * fresh[1:2, :dim], axis=-1, keepdims=True) * factor
    step = lax.broadcasted_iota(jnp.int32, (count, 1), 0) & 1
    new_1 = jnp.where(step == 1, new_1, -1e30)
    top = jnp.maximum(jnp.max(scores, axis=-1, keepdims=True), jnp.maximum(new_0, new_1))
    exp_c = jnp.exp(scores - top)
    exp_0 = jnp.exp(new_0 - top)
    exp_1 = jnp.exp(new_1 - top)
    scale = 1.0 / (jnp.sum(exp_c, axis=-1, keepdims=True) + exp_0 + exp_1)
    weight = (exp_c * scale).astype(BF)
    mixed = jnp.dot(weight, values[0], preferred_element_type=F32)
    mixed = mixed + (exp_0 * scale).astype(BF).astype(F32) * fresh[0:1, dim:]
    mixed = mixed + (exp_1 * scale).astype(BF).astype(F32) * fresh[1:2, dim:]
    mixed = mixed.astype(BF)
    mixed = jnp.concatenate([mixed[h * 32 : (h + 1) * 32] for h in range(heads)], axis=1)
    sub = lax.broadcasted_iota(jnp.int32, (128, 32), 0)
    lane = lax.broadcasted_iota(jnp.int32, (128, 32), 1)
    back = jnp.where(sub == (lane >> 1) * 8 + (lane & 1) * 4 + row, 1.0, 0.0).astype(BF)
    placed = jnp.dot(back, mixed, preferred_element_type=F32)

    @pl.when(row == 0)
    def _():
        acc[...] = placed

    @pl.when(row > 0)
    def _():
        acc[...] += placed

    @pl.when(row == pl.num_programs(0) - 1)
    def _():
        out[...] = acc[...].reshape(16, 8, nq).astype(BF)


def attend(lens, x, keys, values, nq):
    rows, length, dim = keys.shape
    cache = pl.BlockSpec((1, length, dim), lambda r, p: (r, 0, 0))
    return kernel_call(
        attend_body,
        (rows,),
        [whole(x.shape), cache, cache],
        whole((16, 8, nq)),
        jax.ShapeDtypeStruct((16, 8, nq), BF),
        [pltpu.VMEM((128, nq), F32)],
        4 * rows * 96 * length * dim,
        2 * keys.size * 2,
        "attend",
    )(lens, x, keys, values)


def output_body(place, *refs):
    mixed, w_out = refs[:8], refs[8]
    outs, left = refs[9:13], refs[13]
    x, y, z, c = place[0], place[1], place[2], place[3]
    order = one_hot(
        128, 128, lambda o: (o & 64) + ((o >> 2) & 7) * 8 + ((o >> 5) & 1) * 4 + (o & 3)
    )
    for k in range(8):
        bz = (z + k % 4) & 3
        bc = c if k < 4 else 1 - c
        value = mixed[k][...].astype(F32).reshape(128, mixed[k].shape[-1]).astype(BF)
        moved = jnp.dot(order, value, preferred_element_type=F32).astype(BF)
        left[bz * 4 + bc * 2] = moved[:64]
        left[bz * 4 + bc * 2 + 1] = moved[64:]
    mine = jnp.where(c == 0, y, x)
    chunk = w_out.shape[1] // 3
    for d in (2, 1, 3, 0):
        group = (mine + d) & 3
        parts = [left[jnp.where(c == 0, group * 4 + i, i * 4 + group)] for i in range(4)]
        lhs = jnp.concatenate(parts, axis=0)
        for j in range(3):
            cols = pl.ds(j * chunk, chunk)
            outs[d][:, cols] = jnp.dot(
                lhs, w_out[:, cols], preferred_element_type=F32
            ).astype(BF)


def output_partials(place, mixed, w_out):
    depth, width = w_out.shape
    return kernel_call(
        output_body,
        (1,),
        [whole(mixed[0].shape)] * 8 + [whole(w_out.shape)],
        [whole((256, width))] * 4,
        [jax.ShapeDtypeStruct((256, width), BF)] * 4,
        [pltpu.VMEM((16, 64, depth), BF)],
        2 * 1024 * depth * width,
        1024 * depth * 2 + depth * width * 2 + 1024 * width * 2,
        "output_partials",
    )(place, *mixed, w_out)


def group_sum_body(place, a0, a1, a2, a3, own, s1, s2, s3):
    value = a0[...].astype(F32) + a1[...].astype(F32) + a2[...].astype(F32) + a3[...].astype(F32)
    step = pl.program_id(0)

    @pl.when(step == 0)
    def _():
        own[...] = value

    for d, ref in ((1, s1), (2, s2), (3, s3)):

        @pl.when(step == d)
        def _(ref=ref):
            ref[...] = value.astype(BF)


def group_sum(place, parts):
    width = parts[0].shape[-1]
    block = pl.BlockSpec((64, width), lambda d, p: ((jnp.where(p[3] == 0, p[0], p[1]) + d) & 3, 0))
    return kernel_call(
        group_sum_body,
        (4,),
        [block] * 4,
        [whole((64, width))] * 4,
        [jax.ShapeDtypeStruct((64, width), F32)] + [jax.ShapeDtypeStruct((64, width), BF)] * 3,
        [],
        1024 * width,
        1024 * width * 2,
        "group_sum",
    )(place, *parts)


def last_sum_body(place, own, r1, r2, r3, out):
    total = own[...] + r1[...].astype(F32) + r2[...].astype(F32) + r3[...].astype(F32)
    out[...] = total.reshape(out.shape).astype(BF)


def last_sum(place, own, got):
    rows, width = own.shape
    return kernel_call(
        last_sum_body,
        (1,),
        [whole((rows, width))] * 4,
        whole((2, rows // 2, width)),
        jax.ShapeDtypeStruct((2, rows // 2, width), BF),
        [],
        rows * width * 4,
        rows * width * 12,
        "last_sum",
    )(place, own, *got)


def row_statistics(tok, x, y, width_all):
    value = tok.astype(F32)
    count = tok.shape[1]
    mean = jnp.mean(value, axis=-1)
    centred = value - mean[:, None]
    held = jnp.stack([mean, jnp.sum(centred * centred, axis=-1)])
    for place in (
        other_core,
        lambda z, c, y, x: (z ^ 1, c, y, x),
        lambda z, c, y, x: (z ^ 2, c, y, x),
    ):
        other = send(held, place)
        delta = other[0] - held[0]
        held = jnp.stack(
            [(held[0] + other[0]) * 0.5, held[1] + other[1] + delta * delta * (count * 0.5)]
        )
        count = count * 2
    held = jnp.stack([held[0], lax.rsqrt(held[1] / width_all + 1e-05)])[None]
    for bit, place in (
        (x & 1, lambda z, c, y, x: (z, c, y, x ^ 1)),
        (x >> 1, lambda z, c, y, x: (z, c, y, x ^ 2)),
        (y & 1, lambda z, c, y, x: (z, c, y ^ 1, x)),
        (y >> 1, lambda z, c, y, x: (z, c, y ^ 2, x)),
    ):
        other = send(held, place)
        held = jnp.where(
            bit == 1, jnp.concatenate([other, held]), jnp.concatenate([held, other])
        )
    return jnp.swapaxes(held, 1, 2)


def per_device(tokens, norm_gain, w_query, w_kv, w_out, cache_keys, cache_values, lengths):
    gx, gy = lax.axis_index("gx"), lax.axis_index("gy")
    z, c, y, x = gx // 2, gx % 2, gy // 4, gy % 4
    width = tokens.shape[2]
    nq = w_query.shape[1]
    piece = w_kv.shape[1] // 16
    place = jnp.stack([x, y, z, c, c]).astype(jnp.int32)
    place_far = jnp.stack([x, y, z, c, 1 - c]).astype(jnp.int32)

    tok = tokens.reshape(64, width)
    got = [send(tok, first_axis(-1)), send(tok, first_axis(2)), send(tok, first_axis(1))]
    group = jnp.concatenate([tok] + got, axis=0)
    plus = send(group, second_axis(-1))
    minus = send(group, second_axis(1))
    half_a = send(minus[:128], second_axis(1))
    half_b = send(plus[128:], second_axis(-1))
    pieces = (group, plus, minus, half_a, half_b)
    stat = row_statistics(tok, x, y, width * 8)

    gain = norm_gain[None]
    wkv = lax.dynamic_slice_in_dim(w_kv, gy * piece, piece, 1)
    far = project(place_far, pieces, stat, gain, w_query, wkv)
    far_got = send(far, other_core)
    near = project(place, pieces, stat, gain, w_query, wkv)
    own, s1, s2, s3 = pair_sum(place, near, far_got)
    r = [send(s1, z_axis(1)), send(s2, z_axis(2)), send(s3, z_axis(-1))]
    query = finish_query(place, own, r)
    query = lax.all_to_all(query, "gy", 0, 0)
    mixed = attend(lengths, query, cache_keys, cache_values, nq)
    mixed = lax.all_to_all(mixed, "gy", 0, 0)
    same = [mixed, send(mixed, z_axis(-1)), send(mixed, z_axis(2)), send(mixed, z_axis(1))]
    cross = [send(m, other_core) for m in same]
    parts = output_partials(place, same + cross, w_out)
    got = [send(parts[1], second_axis(1)), send(parts[2], second_axis(2)), send(parts[3], second_axis(-1))]
    own, s1, s2, s3 = group_sum(place, [parts[0]] + got)
    got = [send(s1, first_axis(1)), send(s2, first_axis(2)), send(s3, first_axis(-1))]
    return last_sum(place, own, got)


def solution(mesh):
    in_specs = (
        P(None, "gy", "gx"),
        P("gx"),
        P("gx", "gy"),
        P("gx", None),
        P("gy", "gx"),
        P(("gx", "gy"), None, None),
        P(("gx", "gy"), None, None),
        P(("gx", "gy")),
    )
    out_specs = P(None, "gy", "gx")
    return jax.shard_map(
        per_device, mesh=mesh, in_specs=in_specs, out_specs=out_specs, check_vma=False
    )
```

```python
import functools

import jax
import jax.numpy as jnp
from jax import lax
from jax.experimental import pallas as pl
from jax.experimental.pallas import tpu as pltpu
from jax.sharding import PartitionSpec as P

HEADS = 48
BF = jnp.bfloat16
F32 = jnp.float32
VMEM_LIMIT = 20 * 1024 * 1024
ATTEND_VMEM = 57 * 1024 * 1024
PARTIAL_SCALE = 32.0


def flat_perm(place):
    pairs = []
    for gx in range(8):
        for gy in range(16):
            z, c, y, x = gx // 2, gx % 2, gy // 4, gy % 4
            z2, c2, y2, x2 = place(z, c, y, x)
            pairs.append((gx * 16 + gy, ((z2 % 4) * 2 + c2) * 16 + (y2 % 4) * 4 + x2 % 4))
    return pairs


def send(value, place):
    return lax.ppermute(value, ("gx", "gy"), flat_perm(place))


def first_axis(d):
    return lambda z, c, y, x: (z, c, y, x + d) if c == 0 else (z, c, y + d, x)


def second_axis(d):
    return lambda z, c, y, x: (z, c, y + d, x) if c == 0 else (z, c, y, x + d)


def z_axis(d):
    return lambda z, c, y, x: (z + d, c, y, x)


def other_core(z, c, y, x):
    return (z, 1 - c, y, x)


def whole(shape):
    return pl.BlockSpec(shape, lambda *_: (0,) * len(shape))


IN_VMEM = pl.BlockSpec(memory_space=pltpu.VMEM)
IN_SMEM = pl.BlockSpec(memory_space=pltpu.SMEM)
IN_HBM = pl.BlockSpec(memory_space=pltpu.HBM)


def kernel_call(body, grid, in_specs, out_specs, out_shape, scratch, flops, nbytes, name):
    return pl.pallas_call(
        body,
        grid_spec=pltpu.PrefetchScalarGridSpec(
            num_scalar_prefetch=1,
            grid=grid,
            in_specs=in_specs,
            out_specs=out_specs,
            scratch_shapes=scratch,
        ),
        out_shape=out_shape,
        compiler_params=pltpu.CompilerParams(vmem_limit_bytes=VMEM_LIMIT),
        cost_estimate=pl.CostEstimate(flops=flops, bytes_accessed=nbytes, transcendentals=0),
        name=name,
    )


def one_step(body, in_specs, out_shape, scratch, flops, nbytes, name):
    many = isinstance(out_shape, list)
    return pl.pallas_call(
        body,
        in_specs=in_specs,
        out_specs=[IN_VMEM] * len(out_shape) if many else IN_VMEM,
        out_shape=out_shape,
        scratch_shapes=scratch,
        compiler_params=pltpu.CompilerParams(vmem_limit_bytes=VMEM_LIMIT),
        cost_estimate=pl.CostEstimate(flops=flops, bytes_accessed=nbytes, transcendentals=0),
        name=name,
    )


def one_hot(rows, cols, source):
    row = lax.broadcasted_iota(jnp.int32, (rows, cols), 0)
    col = lax.broadcasted_iota(jnp.int32, (rows, cols), 1)
    return jnp.where(col == source(row), 1.0, 0.0).astype(BF)


def one_hot_rows(rows, cols):
    row = lax.broadcasted_iota(jnp.int32, (rows, cols), 0)
    col = lax.broadcasted_iota(jnp.int32, (rows, cols), 1)
    return jnp.where(col % rows == row, 1.0, 0.0).astype(BF)


def row_statistics_body(tok, out):
    value = tok[...].astype(F32)
    rows = value.shape[0]
    mean = jnp.mean(value, axis=-1, keepdims=True)
    centred = value - mean
    squares = jnp.sum(centred * centred, axis=-1, keepdims=True)
    lane = lax.broadcasted_iota(jnp.int32, (rows, 128), 1)
    cols = jnp.where(lane == 0, mean, jnp.where(lane == 1, squares, 0.0))
    cols = jnp.concatenate([cols, jnp.zeros((128 - rows, 128), F32)], axis=0)
    out[0] = jnp.transpose(cols)[:8]


def row_statistics(tok):
    return one_step(
        row_statistics_body,
        [IN_VMEM],
        jax.ShapeDtypeStruct((1, 8, 128), F32),
        [],
        6 * tok.size,
        tok.size * 2,
        "row_statistics",
    )(tok)


def combine(tiles, count, width_all):
    def body(*refs):
        held = [ref[...] for ref in refs[:-1]]
        mean = sum(h[:, 0:1] for h in held) * (1.0 / len(held))
        squares = sum(h[:, 1:2] for h in held)
        spread = sum((h[:, 0:1] - mean) * (h[:, 0:1] - mean) for h in held)
        squares = squares + spread * float(count)
        if width_all:
            squares = lax.rsqrt(squares * (1.0 / width_all) + 1e-05)
        refs[-1][:, 0:1] = mean
        refs[-1][:, 1:2] = squares

    shape = tiles[0].shape
    return one_step(
        body,
        [IN_VMEM] * len(tiles),
        jax.ShapeDtypeStruct(shape, F32),
        [],
        1024 * 10,
        tiles[0].size * 4 * (len(tiles) + 1),
        "combine",
    )(*tiles)


def normalise_body(tok, tile, gain, out):
    cols = jnp.transpose(jnp.concatenate([tile[0], jnp.zeros((120, 128), F32)], axis=0))
    value = tok[...].astype(F32)
    out[...] = ((value - cols[:64, 0:1]) * cols[:64, 1:2] * gain[...]).astype(BF)


def normalise(tok, tile, gain):
    return one_step(
        normalise_body,
        [IN_VMEM] * 3,
        jax.ShapeDtypeStruct(tok.shape, BF),
        [],
        tok.size * 6,
        tok.size * 4,
        "normalise",
    )(tok, tile, gain)


def project_body(places, place, *refs):
    count = len(places)
    halves = refs[: 2 * count]
    wq, wkv = refs[2 * count : 2 * count + 2]
    far, near, rows, sums, sems_in, sems_out = refs[-6:]
    x, y, c = place[0], place[1], place[3]
    nq = wq.shape[1]
    loads = [
        pltpu.make_async_copy(
            ref, rows.at[k // 2, pl.ds((k % 2) * 128, 128)], sems_in.at[k // 2, k % 2]
        )
        for k, ref in enumerate(halves)
    ]
    for copy in loads:
        copy.start()
    for i, d1 in enumerate(places):
        loads[2 * i].wait()
        loads[2 * i + 1].wait()
        sums[i, :, :nq] = jnp.dot(rows[i], wq[...], preferred_element_type=F32)
        sums[i, :, nq:] = jnp.dot(rows[i], wkv[...], preferred_element_type=F32)
        for d2 in range(4):
            bx = (x + jnp.where(c == 0, d2, d1)) & 3
            by = (y + jnp.where(c == 0, d1, d2)) & 3
            slot = by * 2 + (bx & 1)
            source = sums.at[i, pl.ds(d2 * 64, 64)]

            @pl.when((bx >> 1) == c)
            def _(source=source, slot=slot, sem=sems_out.at[i, d2]):
                pltpu.make_async_copy(source, near.at[slot], sem).start()

            @pl.when((bx >> 1) != c)
            def _(source=source, slot=slot, sem=sems_out.at[i, d2]):
                pltpu.make_async_copy(source, far.at[slot], sem).start()

    for i in range(count):
        for d2 in range(4):
            source = sums.at[i, pl.ds(d2 * 64, 64)]
            pltpu.make_async_copy(source, near.at[0], sems_out.at[i, d2]).wait()


def project(places, place, halves, wq, wkv, held):
    width, nq = wq.shape
    n = nq + wkv.shape[1]
    count = len(places)
    rows = 256 * count
    return pl.pallas_call(
        functools.partial(project_body, places),
        in_specs=[IN_SMEM] + [IN_HBM] * (2 * count) + [IN_VMEM] * 2 + [IN_HBM] * len(held),
        out_specs=[IN_HBM] * 2,
        out_shape=[jax.ShapeDtypeStruct((8, 64, n), F32)] * 2,
        scratch_shapes=[
            pltpu.VMEM((count, 256, width), BF),
            pltpu.VMEM((count, 256, n), F32),
            pltpu.SemaphoreType.DMA((count, 2)),
            pltpu.SemaphoreType.DMA((count, 4)),
        ],
        input_output_aliases={2 * count + 3 + i: i for i in range(len(held))},
        compiler_params=pltpu.CompilerParams(vmem_limit_bytes=VMEM_LIMIT),
        cost_estimate=pl.CostEstimate(
            flops=2 * rows * width * n,
            bytes_accessed=rows * width * 2 + width * n * 2 + rows * n * 4,
            transcendentals=0,
        ),
        name="project",
    )(place, *halves, wq, wkv, *held)


def reorder_query_body(total, out):
    order = one_hot(
        128, 128, lambda i: (i & 64) + ((i >> 2) & 1) * 32 + ((i >> 3) & 7) * 4 + (i & 3)
    )
    moved = jnp.dot(order, total[...], preferred_element_type=F32)
    out[...] = moved.reshape(16, 8, moved.shape[-1]).astype(BF)


def reorder_query(total):
    n = total.shape[-1]
    return one_step(
        reorder_query_body,
        [IN_VMEM],
        jax.ShapeDtypeStruct((16, 8, n), BF),
        [],
        2 * 128 * 128 * n,
        128 * n * 4,
        "reorder_query",
    )(total)


def attend_body(lens, x, keys_hbm, values_hbm, out, keys, values, sems):
    nq = out.shape[-1]
    rows, length, dim = keys.shape
    copies = []
    for row in range(rows):
        copies.append(pltpu.make_async_copy(keys_hbm.at[row], keys.at[row], sems.at[0, row]))
        copies.append(pltpu.make_async_copy(values_hbm.at[row], values.at[row], sems.at[1, row]))
    for copy in copies:
        copy.start()
    piece = 2 * dim // 16
    factor = dim ** (-0.5)
    heads = nq // dim
    flat = x[...].astype(F32).reshape(128, x.shape[-1]).astype(BF)

    lane = lax.broadcasted_iota(jnp.int32, (128, 16 * piece), 1)
    sub = lax.broadcasted_iota(jnp.int32, (128, 16 * piece), 0)
    spread = jnp.where((lane % piece == sub) & (sub < piece), 1.0, 0.0).astype(BF)
    tiled = jnp.dot(flat[:, nq : nq + 128], spread, preferred_element_type=F32)
    tiled = jnp.where(lane // piece == sub >> 3, tiled, 0.0).astype(BF)
    fresh = jnp.dot(one_hot_rows(8, 128), tiled, preferred_element_type=F32)

    count = heads * 32
    step = lax.broadcasted_iota(jnp.int32, (count, 1), 0) & 1
    position = lax.broadcasted_iota(jnp.int32, (1, length), 1)
    placed = None
    for row in range(rows):
        if row % 2 == 0:
            for copy in copies[2 * row : 2 * row + 4]:
                copy.wait()
        pick = one_hot(32, 128, lambda i: (i >> 1) * 8 + (i & 1) * 4 + row)
        mine = jnp.dot(pick, flat[:, :nq], preferred_element_type=F32).astype(BF)
        query = jnp.concatenate([mine[:, h * dim : (h + 1) * dim] for h in range(heads)], axis=0)
        scores = (
            lax.dot_general(
                query, keys[row], (((1,), (1,)), ((), ())), preferred_element_type=F32
            )
            * factor
        )
        scores = jnp.where(position < lens[row], scores, -1e30)
        query_f = query.astype(F32)
        key_0, key_1 = fresh[row : row + 1, :dim], fresh[rows + row : rows + row + 1, :dim]
        val_0, val_1 = fresh[row : row + 1, dim:], fresh[rows + row : rows + row + 1, dim:]
        new_0 = jnp.sum(query_f * key_0, axis=-1, keepdims=True) * factor
        new_1 = jnp.sum(query_f * key_1, axis=-1, keepdims=True) * factor
        new_1 = jnp.where(step == 1, new_1, -1e30)
        top = jnp.maximum(jnp.max(scores, axis=-1, keepdims=True), jnp.maximum(new_0, new_1))
        exp_c = jnp.exp(scores - top)
        exp_0 = jnp.exp(new_0 - top)
        exp_1 = jnp.exp(new_1 - top)
        scale = 1.0 / (jnp.sum(exp_c, axis=-1, keepdims=True) + exp_0 + exp_1)
        weight = (exp_c * scale).astype(BF)
        mixed = jnp.dot(weight, values[row], preferred_element_type=F32)
        mixed = mixed + (exp_0 * scale).astype(BF).astype(F32) * val_0
        mixed = mixed + (exp_1 * scale).astype(BF).astype(F32) * val_1
        mixed = mixed.astype(BF)
        mixed = jnp.concatenate([mixed[h * 32 : (h + 1) * 32] for h in range(heads)], axis=1)
        sub = lax.broadcasted_iota(jnp.int32, (128, 32), 0)
        lane = lax.broadcasted_iota(jnp.int32, (128, 32), 1)
        back = jnp.where(sub == (lane >> 1) * 8 + (lane & 1) * 4 + row, 1.0, 0.0).astype(BF)
        term = jnp.dot(back, mixed, preferred_element_type=F32)
        placed = term if placed is None else placed + term
    out[...] = placed.reshape(16, 8, nq).astype(BF)


def attend(lens, x, keys, values, nq):
    rows, length, dim = keys.shape
    return pl.pallas_call(
        attend_body,
        in_specs=[IN_SMEM, IN_VMEM, IN_HBM, IN_HBM],
        out_specs=IN_VMEM,
        out_shape=jax.ShapeDtypeStruct((16, 8, nq), BF),
        scratch_shapes=[
            pltpu.VMEM(keys.shape, BF),
            pltpu.VMEM(values.shape, BF),
            pltpu.SemaphoreType.DMA((2, rows)),
        ],
        compiler_params=pltpu.CompilerParams(vmem_limit_bytes=ATTEND_VMEM),
        cost_estimate=pl.CostEstimate(
            flops=4 * rows * 96 * length * dim, bytes_accessed=4 * keys.size, transcendentals=0
        ),
        name="attend",
    )(lens, x, keys, values)


def output_far_body(place, *refs):
    mixed, w_out = refs[:8], refs[8]
    left, half_a, half_b = refs[9:]
    z, c = place[2], place[3]
    order = one_hot(
        128, 128, lambda o: (o & 64) + ((o >> 2) & 7) * 8 + ((o >> 5) & 1) * 4 + (o & 3)
    )
    for k in range(8):
        bz = (z + k % 4) & 3
        bc = c if k < 4 else 1 - c
        value = mixed[k][...].astype(F32).reshape(128, mixed[k].shape[-1]).astype(BF)
        moved = jnp.dot(order, value, preferred_element_type=F32).astype(BF)
        left[bz * 4 + bc * 2] = moved[:64]
        left[bz * 4 + bc * 2 + 1] = moved[64:]
    partial_rows(place, 2, left, w_out, (half_a, half_b))


def partial_rows(place, d, left, w_out, outs):
    x, y, c = place[0], place[1], place[3]
    group = (jnp.where(c == 0, y, x) + d) & 3
    parts = [left[jnp.where(c == 0, group * 4 + i, i * 4 + group)] for i in range(4)]
    rows = jnp.concatenate(parts, axis=0)
    chunk = w_out.shape[1] // 3
    for j in range(3):
        cols = pl.ds(j * chunk, chunk)
        value = jnp.dot(rows, w_out[:, cols], preferred_element_type=F32).astype(BF)
        at = 0
        for out in outs:
            out[:, cols] = value[at : at + out.shape[0]]
            at += out.shape[0]


def output_far(place, mixed, w_out):
    depth, width = w_out.shape
    return one_step(
        output_far_body,
        [IN_SMEM] + [IN_VMEM] * 9,
        [jax.ShapeDtypeStruct((16, 64, depth), BF)] + [jax.ShapeDtypeStruct((128, width), BF)] * 2,
        [],
        2 * 256 * depth * width,
        1024 * depth * 4 + depth * width * 2 + 256 * width * 2,
        "output_far",
    )(place, *mixed, w_out)


def output_near_body(place, left, w_out, plus_a, plus_b, minus_a, minus_b):
    partial_rows(place, 1, left, w_out, (plus_a, plus_b))
    partial_rows(place, 3, left, w_out, (minus_a, minus_b))


def output_near(place, left, w_out):
    depth, width = w_out.shape
    return one_step(
        output_near_body,
        [IN_SMEM] + [IN_VMEM] * 2,
        [jax.ShapeDtypeStruct((128, width), BF)] * 4,
        [],
        4 * 256 * depth * width,
        1024 * depth * 2 + depth * width * 2 + 512 * width * 2,
        "output_near",
    )(place, left, w_out)


def output_own_body(place, left, w_out, out):
    partial_rows(place, 0, left, w_out, (out,))


def output_own(place, left, w_out):
    depth, width = w_out.shape
    return one_step(
        output_own_body,
        [IN_SMEM] + [IN_VMEM] * 2,
        jax.ShapeDtypeStruct((256, width), BF),
        [],
        2 * 256 * depth * width,
        1024 * depth * 2 + depth * width * 2 + 256 * width * 2,
        "output_own",
    )(place, left, w_out)


def pair_add_body(a0, a1, b0, b1, a, b):
    a[...] = (a0[...].astype(F32) + a1[...].astype(F32)).astype(BF)
    b[...] = (b0[...].astype(F32) + b1[...].astype(F32)).astype(BF)


def pair_add(a0, a1, b0, b1):
    return one_step(
        pair_add_body,
        [IN_VMEM] * 4,
        [jax.ShapeDtypeStruct(a0.shape, BF)] * 2,
        [],
        2 * a0.size,
        a0.size * 12,
        "pair_add",
    )(a0, a1, b0, b1)


def group_sum_body(place, a, b0, b1, c0, c1, own, s1, s2, s3):
    step = pl.program_id(0)
    low = ((jnp.where(place[3] == 0, place[0], place[1]) + step) & 3) < 2
    value = a[...].astype(F32)
    value = value + jnp.where(low, b0[...], b1[...]).astype(F32)
    value = value + jnp.where(low, c0[...], c1[...]).astype(F32)

    @pl.when(step == 0)
    def _():
        own[...] = value

    for d, ref in ((1, s1), (2, s2), (3, s3)):

        @pl.when(step == d)
        def _(ref=ref):
            ref[...] = value.astype(BF)


def group_sum(place, own, halves):
    width = own.shape[-1]
    mine = lambda d, p: (jnp.where(p[3] == 0, p[0], p[1]) + d) & 3
    block = pl.BlockSpec((64, width), lambda d, p: (mine(d, p), 0))
    half = pl.BlockSpec((64, width), lambda d, p: (mine(d, p) & 1, 0))
    return kernel_call(
        group_sum_body,
        (4,),
        [block] + [half] * 4,
        [whole((64, width))] * 4,
        [jax.ShapeDtypeStruct((64, width), F32)] + [jax.ShapeDtypeStruct((64, width), BF)] * 3,
        [],
        1024 * width,
        1024 * width * 2,
        "group_sum",
    )(place, own, *halves)


def last_sum_body(place, own, r1, r2, r3, out):
    total = own[...] + r1[...].astype(F32) + r2[...].astype(F32) + r3[...].astype(F32)
    out[...] = total.reshape(out.shape).astype(BF)


def last_sum(place, own, got):
    rows, width = own.shape
    return one_step(
        last_sum_body,
        [IN_SMEM] + [IN_VMEM] * 4,
        jax.ShapeDtypeStruct((2, rows // 2, width), BF),
        [],
        rows * width * 4,
        rows * width * 12,
        "last_sum",
    )(place, own, *got)


def after(value, other):
    return lax.optimization_barrier((value, other))


def gather_and_project(place, tok, gain, wq, wkv, width_all):
    count = tok.shape[1]
    stat = row_statistics(tok)
    stat = combine([stat, send(stat, other_core)], count, 0)
    stat = combine([stat, send(stat, lambda z, c, y, x: (z ^ 1, c, y, x))], count * 2, 0)
    stat = combine(
        [stat, send(stat, lambda z, c, y, x: (z ^ 2, c, y, x))], count * 4, width_all
    )
    tok = normalise(tok, stat, gain)
    b1, b2, b3 = [send(tok, first_axis(d)) for d in (-1, 2, 1)]
    low = jnp.concatenate([tok, b1], axis=0)
    high = jnp.concatenate([b2, b3], axis=0)
    minus_low = send(low, second_axis(1))
    plus_high = send(high, second_axis(-1))
    minus_high = send(high, second_axis(1))
    plus_low = send(low, second_axis(-1))
    held = project((0,), place, (low, high), wq, wkv, ())
    near, minus_low = after(held[1], minus_low)
    near, plus_high = after(near, plus_high)
    twice_low = send(minus_low, second_axis(1))
    twice_high = send(plus_high, second_axis(-1))
    held = (held[0], near)
    halves = (plus_low, plus_high, minus_low, minus_high)
    held = project((1, 3), place, halves, wq, wkv, held)
    return project((2,), place, (twice_low, twice_high), wq, wkv, held)


def per_device(tokens, norm_gain, w_query, w_kv, w_out, cache_keys, cache_values, lengths):
    gx, gy = lax.axis_index("gx"), lax.axis_index("gy")
    z, c, y, x = gx // 2, gx % 2, gy // 4, gy % 4
    width = tokens.shape[2]
    nq = w_query.shape[1]
    piece = w_kv.shape[1] // 16
    place = jnp.stack([x, y, z, c]).astype(jnp.int32)
    gain = norm_gain[None]
    wkv = lax.dynamic_slice_in_dim(w_kv, gy * piece, piece, 1)
    wkv = jnp.pad(wkv, ((0, 0), (0, 128 - piece)))

    far, near = gather_and_project(
        place, tokens.reshape(64, width), gain, w_query, wkv, width * 8
    )
    n = near.shape[-1]
    far_got = send(far, other_core).reshape(4, 128, n)
    near = near.reshape(4, 128, n)

    def chip_sum(d):
        at = (z + d) & 3
        return lax.dynamic_index_in_dim(near, at, 0, False) + lax.dynamic_index_in_dim(
            far_got, at, 0, False
        )

    got = [
        send((chip_sum(d) * PARTIAL_SCALE).astype(jnp.float16), z_axis(d)) for d in (2, 1, 3)
    ]
    query = chip_sum(0)
    for g in got:
        query = query + g.astype(F32) * (1.0 / PARTIAL_SCALE)
    query = reorder_query(query.astype(BF))
    query = lax.all_to_all(query, "gy", 0, 0)
    mixed = attend(lengths, query, cache_keys, cache_values, nq)
    mixed = lax.all_to_all(mixed, "gy", 0, 0)
    same = [mixed, send(mixed, z_axis(-1)), send(mixed, z_axis(2)), send(mixed, z_axis(1))]
    cross = [send(m, other_core) for m in same]

    left, far_a, far_b = output_far(place, same + cross, w_out)
    got_a = send(far_a, second_axis(1))
    got_b = send(far_b, second_axis(-1))
    plus_a, plus_b, minus_a, minus_b = output_near(place, left, w_out)
    from_minus_b = send(plus_b, second_axis(1))
    from_plus_a = send(minus_a, second_axis(-1))
    own = output_own(place, left, w_out)
    plus_a, minus_b = pair_add(plus_a, got_a, minus_b, got_b)
    from_minus_a = send(plus_a, second_axis(1))
    from_plus_b = send(minus_b, second_axis(-1))
    own, s1, s2, s3 = group_sum(
        place, own, [from_minus_a, from_minus_b, from_plus_a, from_plus_b]
    )
    got = [send(s1, first_axis(1)), send(s2, first_axis(2)), send(s3, first_axis(-1))]
    return last_sum(place, own, got)


def solution(mesh):
    in_specs = (
        P(None, "gy", "gx"),
        P("gx"),
        P("gx", "gy"),
        P("gx", None),
        P("gy", "gx"),
        P(("gx", "gy"), None, None),
        P(("gx", "gy"), None, None),
        P(("gx", "gy")),
    )
    out_specs = P(None, "gy", "gx")
    return jax.shard_map(
        per_device, mesh=mesh, in_specs=in_specs, out_specs=out_specs, check_vma=False
    )
```

```python
import functools

import jax
import jax.numpy as jnp
from jax import lax
from jax.experimental import pallas as pl
from jax.experimental.pallas import tpu as pltpu
from jax.sharding import PartitionSpec as P

HEADS = 48
BF = jnp.bfloat16
F32 = jnp.float32
VMEM_LIMIT = 20 * 1024 * 1024
ATTEND_VMEM = 57 * 1024 * 1024
PARTIAL_SCALE = 32.0


def flat_perm(place):
    pairs = []
    for gx in range(8):
        for gy in range(16):
            z, c, y, x = gx // 2, gx % 2, gy // 4, gy % 4
            z2, c2, y2, x2 = place(z, c, y, x)
            pairs.append((gx * 16 + gy, ((z2 % 4) * 2 + c2) * 16 + (y2 % 4) * 4 + x2 % 4))
    return pairs


def send(value, place):
    return lax.ppermute(value, ("gx", "gy"), flat_perm(place))


def first_axis(d):
    return lambda z, c, y, x: (z, c, y, x + d) if c == 0 else (z, c, y + d, x)


def second_axis(d):
    return lambda z, c, y, x: (z, c, y + d, x) if c == 0 else (z, c, y, x + d)


def z_axis(d):
    return lambda z, c, y, x: (z + d, c, y, x)


def other_core(z, c, y, x):
    return (z, 1 - c, y, x)


def exchange(value):
    groups = [[(2 * z + c) * 16 + g for z in range(4) for g in range(16)] for c in range(2)]
    return lax.all_to_all(value, ("gx", "gy"), 0, 0, axis_index_groups=groups)


def whole(shape):
    return pl.BlockSpec(shape, lambda *_: (0,) * len(shape))


IN_VMEM = pl.BlockSpec(memory_space=pltpu.VMEM)
IN_SMEM = pl.BlockSpec(memory_space=pltpu.SMEM)
IN_HBM = pl.BlockSpec(memory_space=pltpu.HBM)


def kernel_call(body, grid, in_specs, out_specs, out_shape, scratch, flops, nbytes, name):
    return pl.pallas_call(
        body,
        grid_spec=pltpu.PrefetchScalarGridSpec(
            num_scalar_prefetch=1,
            grid=grid,
            in_specs=in_specs,
            out_specs=out_specs,
            scratch_shapes=scratch,
        ),
        out_shape=out_shape,
        compiler_params=pltpu.CompilerParams(vmem_limit_bytes=VMEM_LIMIT),
        cost_estimate=pl.CostEstimate(flops=flops, bytes_accessed=nbytes, transcendentals=0),
        name=name,
    )


def one_step(body, in_specs, out_shape, scratch, flops, nbytes, name):
    many = isinstance(out_shape, list)
    return pl.pallas_call(
        body,
        in_specs=in_specs,
        out_specs=[IN_VMEM] * len(out_shape) if many else IN_VMEM,
        out_shape=out_shape,
        scratch_shapes=scratch,
        compiler_params=pltpu.CompilerParams(vmem_limit_bytes=VMEM_LIMIT),
        cost_estimate=pl.CostEstimate(flops=flops, bytes_accessed=nbytes, transcendentals=0),
        name=name,
    )


def one_hot(rows, cols, source):
    row = lax.broadcasted_iota(jnp.int32, (rows, cols), 0)
    col = lax.broadcasted_iota(jnp.int32, (rows, cols), 1)
    return jnp.where(col == source(row), 1.0, 0.0).astype(BF)


def one_hot_rows(rows, cols):
    row = lax.broadcasted_iota(jnp.int32, (rows, cols), 0)
    col = lax.broadcasted_iota(jnp.int32, (rows, cols), 1)
    return jnp.where(col % rows == row, 1.0, 0.0).astype(BF)


def row_statistics_body(tok, out):
    value = tok[...].astype(F32)
    rows = value.shape[0]
    mean = jnp.mean(value, axis=-1, keepdims=True)
    centred = value - mean
    squares = jnp.sum(centred * centred, axis=-1, keepdims=True)
    lane = lax.broadcasted_iota(jnp.int32, (rows, 128), 1)
    cols = jnp.where(lane == 0, mean, jnp.where(lane == 1, squares, 0.0))
    cols = jnp.concatenate([cols, jnp.zeros((128 - rows, 128), F32)], axis=0)
    out[0] = jnp.transpose(cols)[:8]


def row_statistics(tok):
    return one_step(
        row_statistics_body,
        [IN_VMEM],
        jax.ShapeDtypeStruct((1, 8, 128), F32),
        [],
        6 * tok.size,
        tok.size * 2,
        "row_statistics",
    )(tok)


def combine(tiles, count, width_all):
    def body(*refs):
        held = [ref[...] for ref in refs[:-1]]
        mean = sum(h[:, 0:1] for h in held) * (1.0 / len(held))
        squares = sum(h[:, 1:2] for h in held)
        spread = sum((h[:, 0:1] - mean) * (h[:, 0:1] - mean) for h in held)
        squares = squares + spread * float(count)
        if width_all:
            squares = lax.rsqrt(squares * (1.0 / width_all) + 1e-05)
        refs[-1][:, 0:1] = mean
        refs[-1][:, 1:2] = squares

    shape = tiles[0].shape
    return one_step(
        body,
        [IN_VMEM] * len(tiles),
        jax.ShapeDtypeStruct(shape, F32),
        [],
        1024 * 10,
        tiles[0].size * 4 * (len(tiles) + 1),
        "combine",
    )(*tiles)


def normalise_body(tok, tile, gain, out):
    cols = jnp.transpose(jnp.concatenate([tile[0], jnp.zeros((120, 128), F32)], axis=0))
    value = tok[...].astype(F32)
    value = ((value - cols[:64, 0:1]) * cols[:64, 1:2] * gain[...]).astype(BF)
    order = one_hot(64, 64, lambda o: ((o >> 2) & 1) * 32 + (o >> 3) * 4 + (o & 3))
    out[...] = jnp.dot(order, value, preferred_element_type=F32).astype(BF)


def normalise(tok, tile, gain):
    return one_step(
        normalise_body,
        [IN_VMEM] * 3,
        jax.ShapeDtypeStruct(tok.shape, BF),
        [],
        tok.size * 6,
        tok.size * 4,
        "normalise",
    )(tok, tile, gain)


def project_body(places, place, *refs):
    count = len(places)
    halves = refs[: 2 * count]
    wq, wkv = refs[2 * count : 2 * count + 2]
    far, near, rows, sums, sems_in, sems_out = refs[-6:]
    x, y, c = place[0], place[1], place[3]
    nq = wq.shape[1]
    loads = [
        pltpu.make_async_copy(
            ref, rows.at[k // 2, pl.ds((k % 2) * 128, 128)], sems_in.at[k // 2, k % 2]
        )
        for k, ref in enumerate(halves)
    ]
    for copy in loads:
        copy.start()
    for i, d1 in enumerate(places):
        loads[2 * i].wait()
        loads[2 * i + 1].wait()
        sums[i, :, :nq] = jnp.dot(rows[i], wq[...], preferred_element_type=F32)
        sums[i, :, nq:] = jnp.dot(rows[i], wkv[...], preferred_element_type=F32)
        for d2 in range(4):
            bx = (x + jnp.where(c == 0, d2, d1)) & 3
            by = (y + jnp.where(c == 0, d1, d2)) & 3
            slot = by * 2 + (bx & 1)
            source = sums.at[i, pl.ds(d2 * 64, 64)]

            @pl.when((bx >> 1) == c)
            def _(source=source, slot=slot, sem=sems_out.at[i, d2]):
                pltpu.make_async_copy(source, near.at[slot], sem).start()

            @pl.when((bx >> 1) != c)
            def _(source=source, slot=slot, sem=sems_out.at[i, d2]):
                pltpu.make_async_copy(source, far.at[slot], sem).start()

    for i in range(count):
        for d2 in range(4):
            source = sums.at[i, pl.ds(d2 * 64, 64)]
            pltpu.make_async_copy(source, near.at[0], sems_out.at[i, d2]).wait()


def project(places, place, halves, wq, wkv, held):
    width, nq = wq.shape
    n = nq + wkv.shape[1]
    count = len(places)
    rows = 256 * count
    return pl.pallas_call(
        functools.partial(project_body, places),
        in_specs=[IN_SMEM] + [IN_HBM] * (2 * count) + [IN_VMEM] * 2 + [IN_HBM] * len(held),
        out_specs=[IN_HBM] * 2,
        out_shape=[jax.ShapeDtypeStruct((8, 64, n), F32)] * 2,
        scratch_shapes=[
            pltpu.VMEM((count, 256, width), BF),
            pltpu.VMEM((count, 256, n), F32),
            pltpu.SemaphoreType.DMA((count, 2)),
            pltpu.SemaphoreType.DMA((count, 4)),
        ],
        input_output_aliases={2 * count + 3 + i: i for i in range(len(held))},
        compiler_params=pltpu.CompilerParams(vmem_limit_bytes=VMEM_LIMIT),
        cost_estimate=pl.CostEstimate(
            flops=2 * rows * width * n,
            bytes_accessed=rows * width * 2 + width * n * 2 + rows * n * 4,
            transcendentals=0,
        ),
        name="project",
    )(place, *halves, wq, wkv, *held)


def attend_body(lens, x, keys_hbm, values_hbm, out, keys, values, sems):
    nq = out.shape[-1]
    rows, length, dim = keys.shape
    copies = []
    for row in range(rows):
        copies.append(pltpu.make_async_copy(keys_hbm.at[row], keys.at[row], sems.at[0, row]))
        copies.append(pltpu.make_async_copy(values_hbm.at[row], values.at[row], sems.at[1, row]))
    for copy in copies:
        copy.start()
    piece = 2 * dim // 16
    factor = dim ** (-0.5)
    heads = nq // dim
    flat = x[...].astype(F32).reshape(128, x.shape[-1]).astype(BF)

    lane = lax.broadcasted_iota(jnp.int32, (128, 16 * piece), 1)
    sub = lax.broadcasted_iota(jnp.int32, (128, 16 * piece), 0)
    spread = jnp.where((lane % piece == sub) & (sub < piece), 1.0, 0.0).astype(BF)
    tiled = jnp.dot(flat[:, nq : nq + 128], spread, preferred_element_type=F32)
    tiled = jnp.where(lane // piece == sub >> 3, tiled, 0.0).astype(BF)
    fresh = jnp.dot(one_hot_rows(8, 128), tiled, preferred_element_type=F32)

    count = heads * 32
    step = lax.broadcasted_iota(jnp.int32, (count, 1), 0) & 1
    position = lax.broadcasted_iota(jnp.int32, (1, length), 1)
    placed = None
    for row in range(rows):
        for copy in copies[2 * row : 2 * row + 2]:
            copy.wait()
        pick = one_hot(32, 128, lambda i: (i >> 1) * 8 + (i & 1) * 4 + row)
        mine = jnp.dot(pick, flat[:, :nq], preferred_element_type=F32).astype(BF)
        query = jnp.concatenate([mine[:, h * dim : (h + 1) * dim] for h in range(heads)], axis=0)
        scores = (
            lax.dot_general(
                query, keys[row], (((1,), (1,)), ((), ())), preferred_element_type=F32
            )
            * factor
        )
        scores = jnp.where(position < lens[row], scores, -1e30)
        query_f = query.astype(F32)
        key_0, key_1 = fresh[row : row + 1, :dim], fresh[rows + row : rows + row + 1, :dim]
        val_0, val_1 = fresh[row : row + 1, dim:], fresh[rows + row : rows + row + 1, dim:]
        new_0 = jnp.sum(query_f * key_0, axis=-1, keepdims=True) * factor
        new_1 = jnp.sum(query_f * key_1, axis=-1, keepdims=True) * factor
        new_1 = jnp.where(step == 1, new_1, -1e30)
        top = jnp.maximum(jnp.max(scores, axis=-1, keepdims=True), jnp.maximum(new_0, new_1))
        exp_c = jnp.exp(scores - top)
        exp_0 = jnp.exp(new_0 - top)
        exp_1 = jnp.exp(new_1 - top)
        scale = 1.0 / (jnp.sum(exp_c, axis=-1, keepdims=True) + exp_0 + exp_1)
        weight = (exp_c * scale).astype(BF)
        mixed = jnp.dot(weight, values[row], preferred_element_type=F32)
        mixed = mixed + (exp_0 * scale).astype(BF).astype(F32) * val_0
        mixed = mixed + (exp_1 * scale).astype(BF).astype(F32) * val_1
        mixed = mixed.astype(BF)
        mixed = jnp.concatenate([mixed[h * 32 : (h + 1) * 32] for h in range(heads)], axis=1)
        sub = lax.broadcasted_iota(jnp.int32, (128, 32), 0)
        lane = lax.broadcasted_iota(jnp.int32, (128, 32), 1)
        back = jnp.where(sub == (lane >> 1) * 8 + (lane & 1) * 4 + row, 1.0, 0.0).astype(BF)
        term = jnp.dot(back, mixed, preferred_element_type=F32)
        placed = term if placed is None else placed + term
    placed = placed.reshape(16, 8, nq).astype(BF)
    for copy in range(4):
        out[copy] = placed


def attend(lens, x, keys, values, nq):
    rows, length, dim = keys.shape
    return pl.pallas_call(
        attend_body,
        in_specs=[IN_SMEM, IN_VMEM, IN_HBM, IN_HBM],
        out_specs=IN_VMEM,
        out_shape=jax.ShapeDtypeStruct((4, 16, 8, nq), BF),
        scratch_shapes=[
            pltpu.VMEM(keys.shape, BF),
            pltpu.VMEM(values.shape, BF),
            pltpu.SemaphoreType.DMA((2, rows)),
        ],
        compiler_params=pltpu.CompilerParams(vmem_limit_bytes=ATTEND_VMEM),
        cost_estimate=pl.CostEstimate(
            flops=4 * rows * 96 * length * dim, bytes_accessed=4 * keys.size, transcendentals=0
        ),
        name="attend",
    )(lens, x, keys, values)


def output_far_body(place, same, cross, w_out, left, half_a, half_b):
    c = place[3]
    depth = left.shape[-1]
    for mixed, bc in ((same, c), (cross, 1 - c)):
        for bz in range(4):
            for half in range(2):
                value = mixed[bz, half * 8 : half * 8 + 8].astype(F32)
                left[bz * 4 + bc * 2 + half] = value.reshape(64, depth).astype(BF)
    partial_rows(place, 2, left, w_out, (half_a, half_b))


def partial_rows(place, d, left, w_out, outs):
    x, y, c = place[0], place[1], place[3]
    group = (jnp.where(c == 0, y, x) + d) & 3
    parts = [left[jnp.where(c == 0, group * 4 + i, i * 4 + group)] for i in range(4)]
    rows = jnp.concatenate(parts, axis=0)
    chunk = w_out.shape[1] // 3
    for j in range(3):
        cols = pl.ds(j * chunk, chunk)
        value = jnp.dot(rows, w_out[:, cols], preferred_element_type=F32).astype(BF)
        at = 0
        for out in outs:
            out[:, cols] = value[at : at + out.shape[0]]
            at += out.shape[0]


def output_far(place, same, cross, w_out):
    depth, width = w_out.shape
    return one_step(
        output_far_body,
        [IN_SMEM] + [IN_VMEM] * 3,
        [jax.ShapeDtypeStruct((16, 64, depth), BF)] + [jax.ShapeDtypeStruct((128, width), BF)] * 2,
        [],
        2 * 256 * depth * width,
        1024 * depth * 4 + depth * width * 2 + 256 * width * 2,
        "output_far",
    )(place, same, cross, w_out)


def output_near_body(place, left, w_out, plus_a, plus_b, minus_a, minus_b):
    partial_rows(place, 1, left, w_out, (plus_a, plus_b))
    partial_rows(place, 3, left, w_out, (minus_a, minus_b))


def output_near(place, left, w_out):
    depth, width = w_out.shape
    return one_step(
        output_near_body,
        [IN_SMEM] + [IN_VMEM] * 2,
        [jax.ShapeDtypeStruct((128, width), BF)] * 4,
        [],
        4 * 256 * depth * width,
        1024 * depth * 2 + depth * width * 2 + 512 * width * 2,
        "output_near",
    )(place, left, w_out)


def output_own_body(place, left, w_out, out):
    partial_rows(place, 0, left, w_out, (out,))


def output_own(place, left, w_out):
    depth, width = w_out.shape
    return one_step(
        output_own_body,
        [IN_SMEM] + [IN_VMEM] * 2,
        jax.ShapeDtypeStruct((256, width), BF),
        [],
        2 * 256 * depth * width,
        1024 * depth * 2 + depth * width * 2 + 256 * width * 2,
        "output_own",
    )(place, left, w_out)


def pair_add_body(a0, a1, b0, b1, a, b):
    a[...] = (a0[...].astype(F32) + a1[...].astype(F32)).astype(BF)
    b[...] = (b0[...].astype(F32) + b1[...].astype(F32)).astype(BF)


def pair_add(a0, a1, b0, b1):
    return one_step(
        pair_add_body,
        [IN_VMEM] * 4,
        [jax.ShapeDtypeStruct(a0.shape, BF)] * 2,
        [],
        2 * a0.size,
        a0.size * 12,
        "pair_add",
    )(a0, a1, b0, b1)


def group_sum_body(place, a, b0, b1, c0, c1, own, s1, s2, s3):
    step = pl.program_id(0)
    low = ((jnp.where(place[3] == 0, place[0], place[1]) + step) & 3) < 2
    value = a[...].astype(F32)
    value = value + jnp.where(low, b0[...], b1[...]).astype(F32)
    value = value + jnp.where(low, c0[...], c1[...]).astype(F32)

    @pl.when(step == 0)
    def _():
        own[...] = value

    for d, ref in ((1, s1), (2, s2), (3, s3)):

        @pl.when(step == d)
        def _(ref=ref):
            ref[...] = value.astype(BF)


def group_sum(place, own, halves):
    width = own.shape[-1]
    mine = lambda d, p: (jnp.where(p[3] == 0, p[0], p[1]) + d) & 3
    block = pl.BlockSpec((64, width), lambda d, p: (mine(d, p), 0))
    half = pl.BlockSpec((64, width), lambda d, p: (mine(d, p) & 1, 0))
    return kernel_call(
        group_sum_body,
        (4,),
        [block] + [half] * 4,
        [whole((64, width))] * 4,
        [jax.ShapeDtypeStruct((64, width), F32)] + [jax.ShapeDtypeStruct((64, width), BF)] * 3,
        [],
        1024 * width,
        1024 * width * 2,
        "group_sum",
    )(place, own, *halves)


def last_sum_body(place, own, r1, r2, r3, out):
    total = own[...] + r1[...].astype(F32) + r2[...].astype(F32) + r3[...].astype(F32)
    order = one_hot(64, 64, lambda o: ((o >> 2) & 7) * 8 + (o >> 5) * 4 + (o & 3))
    total = jnp.dot(order, total.astype(BF), preferred_element_type=F32)
    out[...] = total.reshape(out.shape).astype(BF)


def last_sum(place, own, got):
    rows, width = own.shape
    return one_step(
        last_sum_body,
        [IN_SMEM] + [IN_VMEM] * 4,
        jax.ShapeDtypeStruct((2, rows // 2, width), BF),
        [],
        rows * width * 4,
        rows * width * 12,
        "last_sum",
    )(place, own, *got)


def after(value, other):
    return lax.optimization_barrier((value, other))


def gather_and_project(place, tok, gain, wq, wkv, width_all):
    count = tok.shape[1]
    stat = row_statistics(tok)
    stat = combine([stat, send(stat, other_core)], count, 0)
    stat = combine([stat, send(stat, lambda z, c, y, x: (z ^ 1, c, y, x))], count * 2, 0)
    stat = combine(
        [stat, send(stat, lambda z, c, y, x: (z ^ 2, c, y, x))], count * 4, width_all
    )
    tok = normalise(tok, stat, gain)
    b1, b2, b3 = [send(tok, first_axis(d)) for d in (-1, 2, 1)]
    low = jnp.concatenate([tok, b1], axis=0)
    high = jnp.concatenate([b2, b3], axis=0)
    low, high = after(low, high)
    minus_low = send(low, second_axis(1))
    plus_high = send(high, second_axis(-1))
    minus_high = send(high, second_axis(1))
    plus_low = send(low, second_axis(-1))
    held = project((0,), place, (low, high), wq, wkv, ())
    near, minus_low = after(held[1], minus_low)
    near, plus_high = after(near, plus_high)
    twice_low = send(minus_low, second_axis(1))
    twice_high = send(plus_high, second_axis(-1))
    held = (held[0], near)
    halves = (plus_low, plus_high, minus_low, minus_high)
    held = project((1, 3), place, halves, wq, wkv, held)
    return project((2,), place, (twice_low, twice_high), wq, wkv, held)


def per_device(tokens, norm_gain, w_query, w_kv, w_out, cache_keys, cache_values, lengths):
    gx, gy = lax.axis_index("gx"), lax.axis_index("gy")
    z, c, y, x = gx // 2, gx % 2, gy // 4, gy % 4
    width = tokens.shape[2]
    nq = w_query.shape[1]
    piece = w_kv.shape[1] // 16
    place = jnp.stack([x, y, z, c]).astype(jnp.int32)
    gain = norm_gain[None]
    wkv = lax.dynamic_slice_in_dim(w_kv, gy * piece, piece, 1)
    wkv = jnp.pad(wkv, ((0, 0), (0, 128 - piece)))

    far, near = gather_and_project(
        place, tokens.reshape(64, width), gain, w_query, wkv, width * 8
    )
    n = near.shape[-1]

    partial = (near + send(far, other_core)) * PARTIAL_SCALE
    partial = exchange(partial.astype(jnp.float16).reshape(64, 8, n))
    query = jnp.sum(partial.astype(F32).reshape(4, 16, 8, n), axis=0) * (1.0 / PARTIAL_SCALE)
    mixed = attend(lengths, query.astype(BF), cache_keys, cache_values, nq)
    mixed = exchange(mixed.reshape(64, 8, nq)).reshape(4, 16, 8, nq)
    cross = send(mixed, other_core)

    left, far_a, far_b = output_far(place, mixed, cross, w_out)
    got_a = send(far_a, second_axis(1))
    got_b = send(far_b, second_axis(-1))
    plus_a, plus_b, minus_a, minus_b = output_near(place, left, w_out)
    from_minus_b = send(plus_b, second_axis(1))
    from_plus_a = send(minus_a, second_axis(-1))
    own = output_own(place, left, w_out)
    plus_a, minus_b = pair_add(plus_a, got_a, minus_b, got_b)
    from_minus_a = send(plus_a, second_axis(1))
    from_plus_b = send(minus_b, second_axis(-1))
    own, s1, s2, s3 = group_sum(
        place, own, [from_minus_a, from_minus_b, from_plus_a, from_plus_b]
    )
    got = [send(s1, first_axis(1)), send(s2, first_axis(2)), send(s3, first_axis(-1))]
    return last_sum(place, own, got)


def solution(mesh):
    in_specs = (
        P(None, "gy", "gx"),
        P("gx"),
        P("gx", "gy"),
        P("gx", None),
        P("gy", "gx"),
        P(("gx", "gy"), None, None),
        P(("gx", "gy"), None, None),
        P(("gx", "gy")),
    )
    out_specs = P(None, "gy", "gx")
    return jax.shard_map(
        per_device, mesh=mesh, in_specs=in_specs, out_specs=out_specs, check_vma=False
    )
```

```python
import functools

import jax
import jax.numpy as jnp
from jax import lax
from jax.experimental import pallas as pl
from jax.experimental.pallas import tpu as pltpu
from jax.sharding import PartitionSpec as P

HEADS = 48
BF = jnp.bfloat16
F32 = jnp.float32
VMEM_LIMIT = 20 * 1024 * 1024
ATTEND_VMEM = 57 * 1024 * 1024
PARTIAL_SCALE = 32.0


def flat_perm(place):
    pairs = []
    for gx in range(8):
        for gy in range(16):
            z, c, y, x = gx // 2, gx % 2, gy // 4, gy % 4
            z2, c2, y2, x2 = place(z, c, y, x)
            pairs.append((gx * 16 + gy, ((z2 % 4) * 2 + c2) * 16 + (y2 % 4) * 4 + x2 % 4))
    return pairs


def send(value, place):
    return lax.ppermute(value, ("gx", "gy"), flat_perm(place))


def first_axis(d):
    return lambda z, c, y, x: (z, c, y, x + d) if c == 0 else (z, c, y + d, x)


def second_axis(d):
    return lambda z, c, y, x: (z, c, y + d, x) if c == 0 else (z, c, y, x + d)


def z_axis(d):
    return lambda z, c, y, x: (z + d, c, y, x)


def other_core(z, c, y, x):
    return (z, 1 - c, y, x)


def exchange(value):
    groups = [[(2 * z + c) * 16 + g for z in range(4) for g in range(16)] for c in range(2)]
    return lax.all_to_all(value, ("gx", "gy"), 0, 0, axis_index_groups=groups)


def whole(shape):
    return pl.BlockSpec(shape, lambda *_: (0,) * len(shape))


IN_VMEM = pl.BlockSpec(memory_space=pltpu.VMEM)
IN_SMEM = pl.BlockSpec(memory_space=pltpu.SMEM)
IN_HBM = pl.BlockSpec(memory_space=pltpu.HBM)


def kernel_call(body, grid, in_specs, out_specs, out_shape, scratch, flops, nbytes, name):
    return pl.pallas_call(
        body,
        grid_spec=pltpu.PrefetchScalarGridSpec(
            num_scalar_prefetch=1,
            grid=grid,
            in_specs=in_specs,
            out_specs=out_specs,
            scratch_shapes=scratch,
        ),
        out_shape=out_shape,
        compiler_params=pltpu.CompilerParams(vmem_limit_bytes=VMEM_LIMIT),
        cost_estimate=pl.CostEstimate(flops=flops, bytes_accessed=nbytes, transcendentals=0),
        name=name,
    )


def one_step(body, in_specs, out_shape, scratch, flops, nbytes, name):
    many = isinstance(out_shape, list)
    return pl.pallas_call(
        body,
        in_specs=in_specs,
        out_specs=[IN_VMEM] * len(out_shape) if many else IN_VMEM,
        out_shape=out_shape,
        scratch_shapes=scratch,
        compiler_params=pltpu.CompilerParams(vmem_limit_bytes=VMEM_LIMIT),
        cost_estimate=pl.CostEstimate(flops=flops, bytes_accessed=nbytes, transcendentals=0),
        name=name,
    )


def one_hot(rows, cols, source):
    row = lax.broadcasted_iota(jnp.int32, (rows, cols), 0)
    col = lax.broadcasted_iota(jnp.int32, (rows, cols), 1)
    return jnp.where(col == source(row), 1.0, 0.0).astype(BF)


def one_hot_rows(rows, cols):
    row = lax.broadcasted_iota(jnp.int32, (rows, cols), 0)
    col = lax.broadcasted_iota(jnp.int32, (rows, cols), 1)
    return jnp.where(col % rows == row, 1.0, 0.0).astype(BF)


def row_statistics_body(tok, out):
    value = tok[...].astype(F32)
    rows = value.shape[0]
    mean = jnp.mean(value, axis=-1, keepdims=True)
    centred = value - mean
    squares = jnp.sum(centred * centred, axis=-1, keepdims=True)
    lane = lax.broadcasted_iota(jnp.int32, (rows, 128), 1)
    cols = jnp.where(lane == 0, mean, jnp.where(lane == 1, squares, 0.0))
    cols = jnp.concatenate([cols, jnp.zeros((128 - rows, 128), F32)], axis=0)
    tile = jnp.transpose(cols)[:8]
    for k in range(8):
        out[k] = tile


def row_statistics(tok):
    return one_step(
        row_statistics_body,
        [IN_VMEM],
        jax.ShapeDtypeStruct((8, 8, 128), F32),
        [],
        6 * tok.size,
        tok.size * 2,
        "row_statistics",
    )(tok)


def normalise_body(tok, tiles, gain, out):
    count = tok.shape[1]
    held = [tiles[k] for k in range(8)]
    mean = sum(h[0:1] for h in held) * (1.0 / 8)
    squares = sum(h[1:2] + (h[0:1] - mean) * (h[0:1] - mean) * float(count) for h in held)
    inverse = lax.rsqrt(squares * (1.0 / (8 * count)) + 1e-05)
    cols = jnp.transpose(jnp.concatenate([mean, inverse, jnp.zeros((126, 128), F32)], axis=0))
    value = tok[...].astype(F32)
    value = ((value - cols[:64, 0:1]) * cols[:64, 1:2] * gain[...]).astype(BF)
    order = one_hot(64, 64, lambda o: ((o >> 2) & 1) * 32 + (o >> 3) * 4 + (o & 3))
    out[...] = jnp.dot(order, value, preferred_element_type=F32).astype(BF)


def normalise(tok, tiles, gain):
    return one_step(
        normalise_body,
        [IN_VMEM] * 3,
        jax.ShapeDtypeStruct(tok.shape, BF),
        [],
        tok.size * 6,
        tok.size * 4,
        "normalise",
    )(tok, tiles, gain)


def project_body(places, place, *refs):
    count = len(places)
    halves = refs[: 2 * count]
    wq, wkv = refs[2 * count : 2 * count + 2]
    far, near = refs[-2:]
    x, y, c = place[0], place[1], place[3]
    nq = wq.shape[1]
    for k, ref in enumerate(halves):
        d1 = places[k // 2]
        q = jnp.dot(ref[...], wq[...], preferred_element_type=F32)
        kv = jnp.dot(ref[...], wkv[...], preferred_element_type=F32)
        for i in range(2):
            d2 = (k % 2) * 2 + i
            bx = (x + jnp.where(c == 0, d2, d1)) & 3
            by = (y + jnp.where(c == 0, d1, d2)) & 3
            slot = by * 2 + (bx & 1)
            rows = slice(i * 64, i * 64 + 64)
            for out, mine in ((near, (bx >> 1) == c), (far, (bx >> 1) != c)):

                @pl.when(mine)
                def _(out=out, slot=slot, rows=rows, q=q, kv=kv):
                    out[slot, :, :nq] = q[rows]
                    out[slot, :, nq:] = kv[rows]


def project(places, place, halves, wq, wkv, held):
    width, nq = wq.shape
    n = nq + wkv.shape[1]
    count = len(places)
    rows = 256 * count
    return pl.pallas_call(
        functools.partial(project_body, places),
        in_specs=[IN_SMEM] + [IN_VMEM] * (2 * count + 2 + len(held)),
        out_specs=[IN_VMEM] * 2,
        out_shape=[jax.ShapeDtypeStruct((8, 64, n), F32)] * 2,
        input_output_aliases={2 * count + 3 + i: i for i in range(len(held))},
        compiler_params=pltpu.CompilerParams(vmem_limit_bytes=VMEM_LIMIT),
        cost_estimate=pl.CostEstimate(
            flops=2 * rows * width * n,
            bytes_accessed=rows * width * 2 + width * n * 2 + rows * n * 4,
            transcendentals=0,
        ),
        name="project",
    )(place, *halves, wq, wkv, *held)


def attend_body(lens, x, keys_hbm, values_hbm, out, keys, values, sems):
    nq = out.shape[-1]
    rows, length, dim = keys.shape
    key_copies = [
        pltpu.make_async_copy(keys_hbm.at[row], keys.at[row], sems.at[0, row])
        for row in range(rows)
    ]
    value_copies = [
        pltpu.make_async_copy(values_hbm.at[row], values.at[row], sems.at[1, row])
        for row in range(rows)
    ]
    key_copies[0].start()
    for row in range(rows):
        if row + 1 < rows:
            key_copies[row + 1].start()
        value_copies[row].start()
    piece = 2 * dim // 16
    factor = dim ** (-0.5)
    heads = nq // dim
    flat = x[...].astype(F32).reshape(128, x.shape[-1]).astype(BF)

    lane = lax.broadcasted_iota(jnp.int32, (128, 16 * piece), 1)
    sub = lax.broadcasted_iota(jnp.int32, (128, 16 * piece), 0)
    spread = jnp.where((lane % piece == sub) & (sub < piece), 1.0, 0.0).astype(BF)
    tiled = jnp.dot(flat[:, nq : nq + 128], spread, preferred_element_type=F32)
    tiled = jnp.where(lane // piece == sub >> 3, tiled, 0.0).astype(BF)
    fresh = jnp.dot(one_hot_rows(8, 128), tiled, preferred_element_type=F32)

    count = heads * 32
    step = lax.broadcasted_iota(jnp.int32, (count, 1), 0) & 1
    position = lax.broadcasted_iota(jnp.int32, (1, length), 1)

    def scores_of(row):
        pick = one_hot(32, 128, lambda i: (i >> 1) * 8 + (i & 1) * 4 + row)
        mine = jnp.dot(pick, flat[:, :nq], preferred_element_type=F32).astype(BF)
        query = jnp.concatenate([mine[:, h * dim : (h + 1) * dim] for h in range(heads)], axis=0)
        scores = (
            lax.dot_general(
                query, keys[row], (((1,), (1,)), ((), ())), preferred_element_type=F32
            )
            * factor
        )
        scores = jnp.where(position < lens[row], scores, -1e30)
        query_f = query.astype(F32)
        key_0, key_1 = fresh[row : row + 1, :dim], fresh[rows + row : rows + row + 1, :dim]
        new_0 = jnp.sum(query_f * key_0, axis=-1, keepdims=True) * factor
        new_1 = jnp.sum(query_f * key_1, axis=-1, keepdims=True) * factor
        return scores, new_0, jnp.where(step == 1, new_1, -1e30)

    def weights_of(scores, new_0, new_1):
        top = jnp.maximum(jnp.max(scores, axis=-1, keepdims=True), jnp.maximum(new_0, new_1))
        exp_c = jnp.exp(scores - top)
        exp_0 = jnp.exp(new_0 - top)
        exp_1 = jnp.exp(new_1 - top)
        scale = 1.0 / (jnp.sum(exp_c, axis=-1, keepdims=True) + exp_0 + exp_1)
        return (exp_c * scale).astype(BF), (exp_0 * scale).astype(BF), (exp_1 * scale).astype(BF)

    def mix(row, weight, weight_0, weight_1):
        val_0, val_1 = fresh[row : row + 1, dim:], fresh[rows + row : rows + row + 1, dim:]
        mixed = jnp.dot(weight, values[row], preferred_element_type=F32)
        mixed = mixed + weight_0.astype(F32) * val_0 + weight_1.astype(F32) * val_1
        mixed = mixed.astype(BF)
        mixed = jnp.concatenate([mixed[h * 32 : (h + 1) * 32] for h in range(heads)], axis=1)
        sub = lax.broadcasted_iota(jnp.int32, (128, 32), 0)
        lane = lax.broadcasted_iota(jnp.int32, (128, 32), 1)
        back = jnp.where(sub == (lane >> 1) * 8 + (lane & 1) * 4 + row, 1.0, 0.0).astype(BF)
        return jnp.dot(back, mixed, preferred_element_type=F32)

    key_copies[0].wait()
    ahead = scores_of(0)
    placed = jnp.zeros((128, nq), F32)
    for row in range(rows):
        scores = ahead
        if row + 1 < rows:
            key_copies[row + 1].wait()
        value_copies[row].wait()
        if row + 1 < rows:
            ahead = scores_of(row + 1)
        placed = placed + mix(row, *weights_of(*scores))
    placed = placed.reshape(16, 8, nq).astype(BF)
    for copy in range(4):
        out[copy] = placed


def attend(lens, x, keys, values, nq):
    rows, length, dim = keys.shape
    return pl.pallas_call(
        attend_body,
        in_specs=[IN_SMEM, IN_VMEM, IN_HBM, IN_HBM],
        out_specs=IN_VMEM,
        out_shape=jax.ShapeDtypeStruct((4, 16, 8, nq), BF),
        scratch_shapes=[
            pltpu.VMEM(keys.shape, BF),
            pltpu.VMEM(values.shape, BF),
            pltpu.SemaphoreType.DMA((2, rows)),
        ],
        compiler_params=pltpu.CompilerParams(vmem_limit_bytes=ATTEND_VMEM),
        cost_estimate=pl.CostEstimate(
            flops=4 * rows * 96 * length * dim, bytes_accessed=4 * keys.size, transcendentals=0
        ),
        name="attend",
    )(lens, x, keys, values)


def output_far_body(place, same, cross, w_out, left, half_a, half_b):
    c = place[3]
    depth = left.shape[-1]
    for mixed, bc in ((same, c), (cross, 1 - c)):
        for bz in range(4):
            for half in range(2):
                value = mixed[bz, half * 8 : half * 8 + 8].astype(F32)
                left[bz * 4 + bc * 2 + half] = value.reshape(64, depth).astype(BF)
    partial_rows(place, 2, left, w_out, (half_a, half_b))


def partial_rows(place, d, left, w_out, outs):
    x, y, c = place[0], place[1], place[3]
    group = (jnp.where(c == 0, y, x) + d) & 3
    parts = [left[jnp.where(c == 0, group * 4 + i, i * 4 + group)] for i in range(4)]
    rows = jnp.concatenate(parts, axis=0)
    chunk = w_out.shape[1] // 3
    for j in range(3):
        cols = pl.ds(j * chunk, chunk)
        value = jnp.dot(rows, w_out[:, cols], preferred_element_type=F32).astype(BF)
        at = 0
        for out in outs:
            out[:, cols] = value[at : at + out.shape[0]]
            at += out.shape[0]


def output_far(place, same, cross, w_out):
    depth, width = w_out.shape
    return one_step(
        output_far_body,
        [IN_SMEM] + [IN_VMEM] * 3,
        [jax.ShapeDtypeStruct((16, 64, depth), BF)] + [jax.ShapeDtypeStruct((128, width), BF)] * 2,
        [],
        2 * 256 * depth * width,
        1024 * depth * 4 + depth * width * 2 + 256 * width * 2,
        "output_far",
    )(place, same, cross, w_out)


def output_near_body(place, left, w_out, plus_a, plus_b, minus_a, minus_b):
    partial_rows(place, 1, left, w_out, (plus_a, plus_b))
    partial_rows(place, 3, left, w_out, (minus_a, minus_b))


def output_near(place, left, w_out):
    depth, width = w_out.shape
    return one_step(
        output_near_body,
        [IN_SMEM] + [IN_VMEM] * 2,
        [jax.ShapeDtypeStruct((128, width), BF)] * 4,
        [],
        4 * 256 * depth * width,
        1024 * depth * 2 + depth * width * 2 + 512 * width * 2,
        "output_near",
    )(place, left, w_out)


def output_own_body(place, left, w_out, out):
    partial_rows(place, 0, left, w_out, (out,))


def output_own(place, left, w_out):
    depth, width = w_out.shape
    return one_step(
        output_own_body,
        [IN_SMEM] + [IN_VMEM] * 2,
        jax.ShapeDtypeStruct((256, width), BF),
        [],
        2 * 256 * depth * width,
        1024 * depth * 2 + depth * width * 2 + 256 * width * 2,
        "output_own",
    )(place, left, w_out)


def pair_add_body(a0, a1, b0, b1, a, b):
    a[...] = (a0[...].astype(F32) + a1[...].astype(F32)).astype(BF)
    b[...] = (b0[...].astype(F32) + b1[...].astype(F32)).astype(BF)


def pair_add(a0, a1, b0, b1):
    return one_step(
        pair_add_body,
        [IN_VMEM] * 4,
        [jax.ShapeDtypeStruct(a0.shape, BF)] * 2,
        [],
        2 * a0.size,
        a0.size * 12,
        "pair_add",
    )(a0, a1, b0, b1)


def group_sum_body(place, a, b0, b1, c0, c1, own, s1, s2, s3):
    step = pl.program_id(0)
    low = ((jnp.where(place[3] == 0, place[0], place[1]) + step) & 3) < 2
    value = a[...].astype(F32)
    value = value + jnp.where(low, b0[...], b1[...]).astype(F32)
    value = value + jnp.where(low, c0[...], c1[...]).astype(F32)

    @pl.when(step == 0)
    def _():
        own[...] = value

    for d, ref in ((1, s1), (2, s2), (3, s3)):

        @pl.when(step == d)
        def _(ref=ref):
            ref[...] = value.astype(BF)


def group_sum(place, own, halves):
    width = own.shape[-1]
    mine = lambda d, p: (jnp.where(p[3] == 0, p[0], p[1]) + d) & 3
    block = pl.BlockSpec((64, width), lambda d, p: (mine(d, p), 0))
    half = pl.BlockSpec((64, width), lambda d, p: (mine(d, p) & 1, 0))
    return kernel_call(
        group_sum_body,
        (4,),
        [block] + [half] * 4,
        [whole((64, width))] * 4,
        [jax.ShapeDtypeStruct((64, width), F32)] + [jax.ShapeDtypeStruct((64, width), BF)] * 3,
        [],
        1024 * width,
        1024 * width * 2,
        "group_sum",
    )(place, own, *halves)


def last_sum_body(place, own, r1, r2, r3, out):
    total = own[...] + r1[...].astype(F32) + r2[...].astype(F32) + r3[...].astype(F32)
    order = one_hot(64, 64, lambda o: ((o >> 2) & 7) * 8 + (o >> 5) * 4 + (o & 3))
    total = jnp.dot(order, total.astype(BF), preferred_element_type=F32)
    out[...] = total.reshape(out.shape).astype(BF)


def last_sum(place, own, got):
    rows, width = own.shape
    return one_step(
        last_sum_body,
        [IN_SMEM] + [IN_VMEM] * 4,
        jax.ShapeDtypeStruct((2, rows // 2, width), BF),
        [],
        rows * width * 4,
        rows * width * 12,
        "last_sum",
    )(place, own, *got)


def after(value, other):
    return lax.optimization_barrier((value, other))


def gather_and_project(place, tok, gain, wq, wkv):
    stat = lax.all_to_all(row_statistics(tok), "gx", 0, 0)
    tok = normalise(tok, stat, gain)
    b1, b2, b3 = [send(tok, first_axis(d)) for d in (-1, 2, 1)]
    low = jnp.concatenate([tok, b1], axis=0)
    high = jnp.concatenate([b2, b3], axis=0)
    low, high = after(low, high)
    minus_low = send(low, second_axis(1))
    plus_high = send(high, second_axis(-1))
    minus_high = send(high, second_axis(1))
    plus_low = send(low, second_axis(-1))
    held = project((0,), place, (low, high), wq, wkv, ())
    near, minus_low = after(held[1], minus_low)
    near, plus_high = after(near, plus_high)
    twice_low = send(minus_low, second_axis(1))
    twice_high = send(plus_high, second_axis(-1))
    held = (held[0], near)
    halves = (plus_low, plus_high, minus_low, minus_high)
    held = project((1, 3), place, halves, wq, wkv, held)
    return project((2,), place, (twice_low, twice_high), wq, wkv, held)


def per_device(tokens, norm_gain, w_query, w_kv, w_out, cache_keys, cache_values, lengths):
    gx, gy = lax.axis_index("gx"), lax.axis_index("gy")
    z, c, y, x = gx // 2, gx % 2, gy // 4, gy % 4
    width = tokens.shape[2]
    nq = w_query.shape[1]
    piece = w_kv.shape[1] // 16
    place = jnp.stack([x, y, z, c]).astype(jnp.int32)
    gain = norm_gain[None]
    wkv = lax.dynamic_slice_in_dim(w_kv, gy * piece, piece, 1)
    wkv = jnp.pad(wkv, ((0, 0), (0, 128 - piece)))

    far, near = gather_and_project(
        place, tokens.reshape(64, width), gain, w_query, wkv
    )
    n = near.shape[-1]

    partial = (near + send(far, other_core)) * PARTIAL_SCALE
    partial = exchange(partial.astype(jnp.float16).reshape(64, 8, n))
    query = jnp.sum(partial.astype(F32).reshape(4, 16, 8, n), axis=0) * (1.0 / PARTIAL_SCALE)
    mixed = attend(lengths, query.astype(BF), cache_keys, cache_values, nq)
    mixed = exchange(mixed.reshape(64, 8, nq)).reshape(4, 16, 8, nq)
    cross = send(mixed, other_core)

    left, far_a, far_b = output_far(place, mixed, cross, w_out)
    got_a = send(far_a, second_axis(1))
    got_b = send(far_b, second_axis(-1))
    plus_a, plus_b, minus_a, minus_b = output_near(place, left, w_out)
    from_minus_b = send(plus_b, second_axis(1))
    from_plus_a = send(minus_a, second_axis(-1))
    own = output_own(place, left, w_out)
    plus_a, minus_b = pair_add(plus_a, got_a, minus_b, got_b)
    from_minus_a = send(plus_a, second_axis(1))
    from_plus_b = send(minus_b, second_axis(-1))
    own, s1, s2, s3 = group_sum(
        place, own, [from_minus_a, from_minus_b, from_plus_a, from_plus_b]
    )
    got = [send(s1, first_axis(1)), send(s2, first_axis(2)), send(s3, first_axis(-1))]
    return last_sum(place, own, got)


def solution(mesh):
    in_specs = (
        P(None, "gy", "gx"),
        P("gx"),
        P("gx", "gy"),
        P("gx", None),
        P("gy", "gx"),
        P(("gx", "gy"), None, None),
        P(("gx", "gy"), None, None),
        P(("gx", "gy")),
    )
    out_specs = P(None, "gy", "gx")
    return jax.shard_map(
        per_device, mesh=mesh, in_specs=in_specs, out_specs=out_specs, check_vma=False
    )
```

```python
import functools

import jax
import jax.numpy as jnp
from jax import lax
from jax.experimental import pallas as pl
from jax.experimental.pallas import tpu as pltpu
from jax.sharding import PartitionSpec as P

HEADS = 48
BF = jnp.bfloat16
F32 = jnp.float32
VMEM_LIMIT = 20 * 1024 * 1024
ATTEND_VMEM = 57 * 1024 * 1024
PARTIAL_SCALE = 32.0


def flat_perm(place):
    pairs = []
    for gx in range(8):
        for gy in range(16):
            z, c, y, x = gx // 2, gx % 2, gy // 4, gy % 4
            z2, c2, y2, x2 = place(z, c, y, x)
            pairs.append((gx * 16 + gy, ((z2 % 4) * 2 + c2) * 16 + (y2 % 4) * 4 + x2 % 4))
    return pairs


def send(value, place):
    return lax.ppermute(value, ("gx", "gy"), flat_perm(place))


def first_axis(d):
    return lambda z, c, y, x: (z, c, y, x + d) if c == 0 else (z, c, y + d, x)


def second_axis(d):
    return lambda z, c, y, x: (z, c, y + d, x) if c == 0 else (z, c, y, x + d)


def z_axis(d):
    return lambda z, c, y, x: (z + d, c, y, x)


def other_core(z, c, y, x):
    return (z, 1 - c, y, x)


def exchange(value):
    groups = [[(2 * z + c) * 16 + g for z in range(4) for g in range(16)] for c in range(2)]
    return lax.all_to_all(value, ("gx", "gy"), 0, 0, axis_index_groups=groups)


IN_VMEM = pl.BlockSpec(memory_space=pltpu.VMEM)
IN_SMEM = pl.BlockSpec(memory_space=pltpu.SMEM)
IN_HBM = pl.BlockSpec(memory_space=pltpu.HBM)


def one_step(body, in_specs, out_shape, scratch, flops, nbytes, name):
    many = isinstance(out_shape, list)
    return pl.pallas_call(
        body,
        in_specs=in_specs,
        out_specs=[IN_VMEM] * len(out_shape) if many else IN_VMEM,
        out_shape=out_shape,
        scratch_shapes=scratch,
        compiler_params=pltpu.CompilerParams(vmem_limit_bytes=VMEM_LIMIT),
        cost_estimate=pl.CostEstimate(flops=flops, bytes_accessed=nbytes, transcendentals=0),
        name=name,
    )


def one_hot(rows, cols, source):
    row = lax.broadcasted_iota(jnp.int32, (rows, cols), 0)
    col = lax.broadcasted_iota(jnp.int32, (rows, cols), 1)
    return jnp.where(col == source(row), 1.0, 0.0).astype(BF)


def one_hot_rows(rows, cols):
    row = lax.broadcasted_iota(jnp.int32, (rows, cols), 0)
    col = lax.broadcasted_iota(jnp.int32, (rows, cols), 1)
    return jnp.where(col % rows == row, 1.0, 0.0).astype(BF)


def row_statistics_body(tok, out):
    value = tok[...].astype(F32)
    rows = value.shape[0]
    mean = jnp.mean(value, axis=-1, keepdims=True)
    centred = value - mean
    squares = jnp.sum(centred * centred, axis=-1, keepdims=True)
    lane = lax.broadcasted_iota(jnp.int32, (rows, 128), 1)
    cols = jnp.where(lane == 0, mean, jnp.where(lane == 1, squares, 0.0))
    cols = jnp.concatenate([cols, jnp.zeros((128 - rows, 128), F32)], axis=0)
    out[...] = jnp.transpose(cols)[:8]


def row_statistics(tok):
    return one_step(
        row_statistics_body,
        [IN_VMEM],
        jax.ShapeDtypeStruct((8, 128), F32),
        [],
        6 * tok.size,
        tok.size * 2,
        "row_statistics",
    )(tok)


def join(tiles, count):
    mean = sum(t[0:1] for t in tiles) * (1.0 / len(tiles))
    squares = sum(t[1:2] + (t[0:1] - mean) * (t[0:1] - mean) * float(count) for t in tiles)
    return mean, squares


def chip_statistics(mine, other, count):
    def body(a, b, out):
        mean, squares = join([a[...], b[...]], count)
        tile = jnp.concatenate([mean, squares, jnp.zeros((6, 128), F32)], axis=0)
        for k in range(16):
            out[k] = tile

    return one_step(
        body,
        [IN_VMEM] * 2,
        jax.ShapeDtypeStruct((16, 8, 128), F32),
        [],
        16 * 1024,
        18 * 4096,
        "chip_statistics",
    )(mine, other)


def normalise_body(place, b0, b1, b2, b3, tiles, gain, low, high):
    me = jnp.where(place[3] == 0, place[0], place[1])
    count = b0.shape[1]
    order = one_hot(64, 64, lambda o: ((o >> 2) & 1) * 32 + (o >> 3) * 4 + (o & 3))
    for k, block in enumerate((b0, b1, b2, b3)):
        mean, squares = join([tiles[4 * z + ((me + k) & 3)] for z in range(4)], 2 * count)
        inverse = lax.rsqrt(squares * (1.0 / (8 * count)) + 1e-05)
        cols = jnp.transpose(
            jnp.concatenate([mean, inverse, jnp.zeros((126, 128), F32)], axis=0)
        )
        value = block[...].astype(F32)
        value = ((value - cols[:64, 0:1]) * cols[:64, 1:2] * gain[...]).astype(BF)
        value = jnp.dot(order, value, preferred_element_type=F32).astype(BF)
        (low, high)[k // 2][(k % 2) * 64 : (k % 2) * 64 + 64] = value


def normalise(place, blocks, tiles, gain):
    width = blocks[0].shape[1]
    return one_step(
        normalise_body,
        [IN_SMEM] + [IN_VMEM] * 6,
        [jax.ShapeDtypeStruct((128, width), BF)] * 2,
        [],
        256 * width * 6,
        256 * width * 4,
        "normalise",
    )(place, *blocks, tiles, gain)


def project_body(places, place, *refs):
    count = len(places)
    halves = refs[: 2 * count]
    wq, wkv = refs[2 * count : 2 * count + 2]
    far, near = refs[-2:]
    x, y, c = place[0], place[1], place[3]
    nq = wq.shape[1]
    for k, ref in enumerate(halves):
        d1 = places[k // 2]
        q = jnp.dot(ref[...], wq[...], preferred_element_type=F32)
        kv = jnp.dot(ref[...], wkv[...], preferred_element_type=F32)
        for i in range(2):
            d2 = (k % 2) * 2 + i
            bx = (x + jnp.where(c == 0, d2, d1)) & 3
            by = (y + jnp.where(c == 0, d1, d2)) & 3
            slot = by * 2 + (bx & 1)
            rows = slice(i * 64, i * 64 + 64)
            for out, mine in ((near, (bx >> 1) == c), (far, (bx >> 1) != c)):

                @pl.when(mine)
                def _(out=out, slot=slot, rows=rows, q=q, kv=kv):
                    out[slot, :, :nq] = q[rows]
                    out[slot, :, nq:] = kv[rows]


def project(places, place, halves, wq, wkv, held):
    width, nq = wq.shape
    n = nq + wkv.shape[1]
    count = len(places)
    rows = 256 * count
    return pl.pallas_call(
        functools.partial(project_body, places),
        in_specs=[IN_SMEM] + [IN_VMEM] * (2 * count + 2 + len(held)),
        out_specs=[IN_VMEM] * 2,
        out_shape=[jax.ShapeDtypeStruct((8, 64, n), F32)] * 2,
        input_output_aliases={2 * count + 3 + i: i for i in range(len(held))},
        compiler_params=pltpu.CompilerParams(vmem_limit_bytes=VMEM_LIMIT),
        cost_estimate=pl.CostEstimate(
            flops=2 * rows * width * n,
            bytes_accessed=rows * width * 2 + width * n * 2 + rows * n * 4,
            transcendentals=0,
        ),
        name="project",
    )(place, *halves, wq, wkv, *held)


def attend_body(lens, x, keys_hbm, values_hbm, out, keys, values, sems):
    nq = out.shape[-1]
    rows, length, dim = keys.shape
    key_copies = [
        pltpu.make_async_copy(keys_hbm.at[row], keys.at[row], sems.at[0, row])
        for row in range(rows)
    ]
    value_copies = [
        pltpu.make_async_copy(values_hbm.at[row], values.at[row], sems.at[1, row])
        for row in range(rows)
    ]
    key_copies[0].start()
    for row in range(rows):
        if row + 1 < rows:
            key_copies[row + 1].start()
        value_copies[row].start()
    piece = 2 * dim // 16
    factor = dim ** (-0.5)
    heads = nq // dim
    flat = x[...].astype(F32).reshape(128, x.shape[-1]).astype(BF)

    lane = lax.broadcasted_iota(jnp.int32, (128, 16 * piece), 1)
    sub = lax.broadcasted_iota(jnp.int32, (128, 16 * piece), 0)
    spread = jnp.where((lane % piece == sub) & (sub < piece), 1.0, 0.0).astype(BF)
    tiled = jnp.dot(flat[:, nq : nq + 128], spread, preferred_element_type=F32)
    tiled = jnp.where(lane // piece == sub >> 3, tiled, 0.0).astype(BF)
    fresh = jnp.dot(one_hot_rows(8, 128), tiled, preferred_element_type=F32)

    count = heads * 32
    step = lax.broadcasted_iota(jnp.int32, (count, 1), 0) & 1
    position = lax.broadcasted_iota(jnp.int32, (1, length), 1)

    def scores_of(row):
        pick = one_hot(32, 128, lambda i: (i >> 1) * 8 + (i & 1) * 4 + row)
        mine = jnp.dot(pick, flat[:, :nq], preferred_element_type=F32).astype(BF)
        query = jnp.concatenate([mine[:, h * dim : (h + 1) * dim] for h in range(heads)], axis=0)
        scores = (
            lax.dot_general(
                query, keys[row], (((1,), (1,)), ((), ())), preferred_element_type=F32
            )
            * factor
        )
        scores = jnp.where(position < lens[row], scores, -1e30)
        query_f = query.astype(F32)
        key_0, key_1 = fresh[row : row + 1, :dim], fresh[rows + row : rows + row + 1, :dim]
        new_0 = jnp.sum(query_f * key_0, axis=-1, keepdims=True) * factor
        new_1 = jnp.sum(query_f * key_1, axis=-1, keepdims=True) * factor
        return scores, new_0, jnp.where(step == 1, new_1, -1e30)

    def weights_of(scores, new_0, new_1):
        top = jnp.maximum(jnp.max(scores, axis=-1, keepdims=True), jnp.maximum(new_0, new_1))
        exp_c = jnp.exp(scores - top)
        exp_0 = jnp.exp(new_0 - top)
        exp_1 = jnp.exp(new_1 - top)
        scale = 1.0 / (jnp.sum(exp_c, axis=-1, keepdims=True) + exp_0 + exp_1)
        return (exp_c * scale).astype(BF), (exp_0 * scale).astype(BF), (exp_1 * scale).astype(BF)

    def mix(row, weight, weight_0, weight_1):
        val_0, val_1 = fresh[row : row + 1, dim:], fresh[rows + row : rows + row + 1, dim:]
        mixed = jnp.dot(weight, values[row], preferred_element_type=F32)
        mixed = mixed + weight_0.astype(F32) * val_0 + weight_1.astype(F32) * val_1
        mixed = mixed.astype(BF)
        mixed = jnp.concatenate([mixed[h * 32 : (h + 1) * 32] for h in range(heads)], axis=1)
        sub = lax.broadcasted_iota(jnp.int32, (128, 32), 0)
        lane = lax.broadcasted_iota(jnp.int32, (128, 32), 1)
        back = jnp.where(sub == (lane >> 1) * 8 + (lane & 1) * 4 + row, 1.0, 0.0).astype(BF)
        return jnp.dot(back, mixed, preferred_element_type=F32)

    key_copies[0].wait()
    ahead = scores_of(0)
    placed = jnp.zeros((128, nq), F32)
    for row in range(rows):
        scores = ahead
        if row + 1 < rows:
            key_copies[row + 1].wait()
        value_copies[row].wait()
        if row + 1 < rows:
            ahead = scores_of(row + 1)
        placed = placed + mix(row, *weights_of(*scores))
    placed = placed.reshape(16, 8, nq).astype(BF)
    for copy in range(4):
        out[copy] = placed


def attend(lens, x, keys, values, nq):
    rows, length, dim = keys.shape
    return pl.pallas_call(
        attend_body,
        in_specs=[IN_SMEM, IN_VMEM, IN_HBM, IN_HBM],
        out_specs=IN_VMEM,
        out_shape=jax.ShapeDtypeStruct((4, 16, 8, nq), BF),
        scratch_shapes=[
            pltpu.VMEM(keys.shape, BF),
            pltpu.VMEM(values.shape, BF),
            pltpu.SemaphoreType.DMA((2, rows)),
        ],
        compiler_params=pltpu.CompilerParams(vmem_limit_bytes=ATTEND_VMEM),
        cost_estimate=pl.CostEstimate(
            flops=4 * rows * 96 * length * dim, bytes_accessed=4 * keys.size, transcendentals=0
        ),
        name="attend",
    )(lens, x, keys, values)


def output_far_body(place, same, cross, w_out, left, half_a, half_b):
    c = place[3]
    depth = left.shape[-1]
    for mixed, bc in ((same, c), (cross, 1 - c)):
        for bz in range(4):
            for half in range(2):
                value = mixed[bz, half * 8 : half * 8 + 8].astype(F32)
                left[bz * 4 + bc * 2 + half] = value.reshape(64, depth).astype(BF)
    partial_rows(place, 2, left, w_out, (half_a, half_b))


def partial_rows(place, d, left, w_out, outs):
    x, y, c = place[0], place[1], place[3]
    group = (jnp.where(c == 0, y, x) + d) & 3
    parts = [left[jnp.where(c == 0, group * 4 + i, i * 4 + group)] for i in range(4)]
    rows = jnp.concatenate(parts, axis=0)
    chunk = w_out.shape[1] // 3
    for j in range(3):
        cols = pl.ds(j * chunk, chunk)
        value = jnp.dot(rows, w_out[:, cols], preferred_element_type=F32).astype(BF)
        at = 0
        for out in outs:
            out[:, cols] = value[at : at + out.shape[0]]
            at += out.shape[0]


def output_far(place, same, cross, w_out):
    depth, width = w_out.shape
    return one_step(
        output_far_body,
        [IN_SMEM] + [IN_VMEM] * 3,
        [jax.ShapeDtypeStruct((16, 64, depth), BF)] + [jax.ShapeDtypeStruct((128, width), BF)] * 2,
        [],
        2 * 256 * depth * width,
        1024 * depth * 4 + depth * width * 2 + 256 * width * 2,
        "output_far",
    )(place, same, cross, w_out)


def output_near_body(place, left, w_out, plus_a, plus_b, minus_a, minus_b):
    partial_rows(place, 1, left, w_out, (plus_a, plus_b))
    partial_rows(place, 3, left, w_out, (minus_a, minus_b))


def output_near(place, left, w_out):
    depth, width = w_out.shape
    return one_step(
        output_near_body,
        [IN_SMEM] + [IN_VMEM] * 2,
        [jax.ShapeDtypeStruct((128, width), BF)] * 4,
        [],
        4 * 256 * depth * width,
        1024 * depth * 2 + depth * width * 2 + 512 * width * 2,
        "output_near",
    )(place, left, w_out)


def output_own_body(place, left, w_out, out):
    partial_rows(place, 0, left, w_out, (out,))


def output_own(place, left, w_out):
    depth, width = w_out.shape
    return one_step(
        output_own_body,
        [IN_SMEM] + [IN_VMEM] * 2,
        jax.ShapeDtypeStruct((256, width), BF),
        [],
        2 * 256 * depth * width,
        1024 * depth * 2 + depth * width * 2 + 256 * width * 2,
        "output_own",
    )(place, left, w_out)


def pair_add_body(a0, a1, b0, b1, a, b):
    a[...] = (a0[...].astype(F32) + a1[...].astype(F32)).astype(BF)
    b[...] = (b0[...].astype(F32) + b1[...].astype(F32)).astype(BF)


def pair_add(a0, a1, b0, b1):
    return one_step(
        pair_add_body,
        [IN_VMEM] * 4,
        [jax.ShapeDtypeStruct(a0.shape, BF)] * 2,
        [],
        2 * a0.size,
        a0.size * 12,
        "pair_add",
    )(a0, a1, b0, b1)


def group_sum_body(place, a, b0, b1, c0, c1, own, s1, s2, s3):
    me = jnp.where(place[3] == 0, place[0], place[1])
    for d, out in enumerate((own, s1, s2, s3)):
        at = (me + d) & 3
        half = pl.ds(pl.multiple_of((at & 1) * 64, 64), 64)
        value = a[pl.ds(pl.multiple_of(at * 64, 64), 64)].astype(F32)
        value = value + jnp.where(at < 2, b0[half], b1[half]).astype(F32)
        value = value + jnp.where(at < 2, c0[half], c1[half]).astype(F32)
        out[...] = value.astype(out.dtype)


def group_sum(place, own, halves):
    width = own.shape[-1]
    return one_step(
        group_sum_body,
        [IN_SMEM] + [IN_VMEM] * 5,
        [jax.ShapeDtypeStruct((64, width), F32)] + [jax.ShapeDtypeStruct((64, width), BF)] * 3,
        [],
        1024 * width,
        1024 * width * 2,
        "group_sum",
    )(place, own, *halves)


def last_sum_body(place, own, r1, r2, r3, out):
    total = own[...] + r1[...].astype(F32) + r2[...].astype(F32) + r3[...].astype(F32)
    order = one_hot(64, 64, lambda o: ((o >> 2) & 7) * 8 + (o >> 5) * 4 + (o & 3))
    total = jnp.dot(order, total.astype(BF), preferred_element_type=F32)
    out[...] = total.reshape(out.shape).astype(BF)


def last_sum(place, own, got):
    rows, width = own.shape
    return one_step(
        last_sum_body,
        [IN_SMEM] + [IN_VMEM] * 4,
        jax.ShapeDtypeStruct((2, rows // 2, width), BF),
        [],
        rows * width * 4,
        rows * width * 12,
        "last_sum",
    )(place, own, *got)


def after(value, other):
    return lax.optimization_barrier((value, other))


def gather_and_project(place, tok, gain, wq, wkv):
    stat = row_statistics(tok)
    b1, b3, b2 = [send(tok, first_axis(d)) for d in (-1, 1, 2)]
    blocks = [tok, b1, b2, b3]
    stat = chip_statistics(stat, send(stat, other_core), tok.shape[1])
    groups = [[2 * z * 16 + 4 * i + j for z in range(4) for j in range(4)] for i in range(4)]
    groups += [
        [(2 * z + 1) * 16 + 4 * j + i for z in range(4) for j in range(4)] for i in range(4)
    ]
    tiles = lax.all_to_all(stat, ("gx", "gy"), 0, 0, axis_index_groups=groups)
    low, high = normalise(place, blocks, tiles, gain)
    minus_low = send(low, second_axis(1))
    plus_high = send(high, second_axis(-1))
    minus_high = send(high, second_axis(1))
    plus_low = send(low, second_axis(-1))
    held = project((0,), place, (low, high), wq, wkv, ())
    near, minus_low = after(held[1], minus_low)
    near, plus_high = after(near, plus_high)
    twice_low = send(minus_low, second_axis(1))
    twice_high = send(plus_high, second_axis(-1))
    held = (held[0], near)
    halves = (plus_low, plus_high, minus_low, minus_high)
    held = project((1, 3), place, halves, wq, wkv, held)
    return project((2,), place, (twice_low, twice_high), wq, wkv, held)


def per_device(tokens, norm_gain, w_query, w_kv, w_out, cache_keys, cache_values, lengths):
    gx, gy = lax.axis_index("gx"), lax.axis_index("gy")
    z, c, y, x = gx // 2, gx % 2, gy // 4, gy % 4
    width = tokens.shape[2]
    nq = w_query.shape[1]
    piece = w_kv.shape[1] // 16
    place = jnp.stack([x, y, z, c]).astype(jnp.int32)
    gain = norm_gain[None]
    wkv = lax.dynamic_slice_in_dim(w_kv, gy * piece, piece, 1)
    wkv = jnp.pad(wkv, ((0, 0), (0, 128 - piece)))

    far, near = gather_and_project(
        place, tokens.reshape(64, width), gain, w_query, wkv
    )
    n = near.shape[-1]

    partial = (near + send(far, other_core)) * PARTIAL_SCALE
    partial = exchange(partial.astype(jnp.float16).reshape(64, 8, n))
    query = jnp.sum(partial.astype(F32).reshape(4, 16, 8, n), axis=0) * (1.0 / PARTIAL_SCALE)
    mixed = attend(lengths, query.astype(BF), cache_keys, cache_values, nq)
    mixed = exchange(mixed.reshape(64, 8, nq)).reshape(4, 16, 8, nq)
    cross = send(mixed, other_core)

    left, far_a, far_b = output_far(place, mixed, cross, w_out)
    got_a = send(far_a, second_axis(1))
    got_b = send(far_b, second_axis(-1))
    plus_a, plus_b, minus_a, minus_b = output_near(place, left, w_out)
    from_minus_b = send(plus_b, second_axis(1))
    from_plus_a = send(minus_a, second_axis(-1))
    own = output_own(place, left, w_out)
    plus_a, minus_b = pair_add(plus_a, got_a, minus_b, got_b)
    from_minus_a = send(plus_a, second_axis(1))
    from_plus_b = send(minus_b, second_axis(-1))
    own, s1, s2, s3 = group_sum(
        place, own, [from_minus_a, from_minus_b, from_plus_a, from_plus_b]
    )
    got = [send(s2, first_axis(2)), send(s1, first_axis(1)), send(s3, first_axis(-1))]
    return last_sum(place, own, got)


def solution(mesh):
    in_specs = (
        P(None, "gy", "gx"),
        P("gx"),
        P("gx", "gy"),
        P("gx", None),
        P("gy", "gx"),
        P(("gx", "gy"), None, None),
        P(("gx", "gy"), None, None),
        P(("gx", "gy")),
    )
    out_specs = P(None, "gy", "gx")
    return jax.shard_map(
        per_device, mesh=mesh, in_specs=in_specs, out_specs=out_specs, check_vma=False
    )
```

```python
import functools

import jax
import jax.numpy as jnp
from jax import lax
from jax.experimental import pallas as pl
from jax.experimental.pallas import tpu as pltpu
from jax.sharding import PartitionSpec as P

HEADS = 48
BF = jnp.bfloat16
F32 = jnp.float32
VMEM_LIMIT = 20 * 1024 * 1024
ATTEND_VMEM = 57 * 1024 * 1024
PARTIAL_SCALE = 32.0


def flat_perm(place):
    pairs = []
    for gx in range(8):
        for gy in range(16):
            z, c, y, x = gx // 2, gx % 2, gy // 4, gy % 4
            z2, c2, y2, x2 = place(z, c, y, x)
            pairs.append((gx * 16 + gy, ((z2 % 4) * 2 + c2) * 16 + (y2 % 4) * 4 + x2 % 4))
    return pairs


def send(value, place):
    return lax.ppermute(value, ("gx", "gy"), flat_perm(place))


def first_axis(d):
    return lambda z, c, y, x: (z, c, y, x + d) if c == 0 else (z, c, y + d, x)


def second_axis(d):
    return lambda z, c, y, x: (z, c, y + d, x) if c == 0 else (z, c, y, x + d)


def z_axis(d):
    return lambda z, c, y, x: (z + d, c, y, x)


def other_core(z, c, y, x):
    return (z, 1 - c, y, x)


def exchange(value):
    groups = [[(2 * z + c) * 16 + g for z in range(4) for g in range(16)] for c in range(2)]
    return lax.all_to_all(value, ("gx", "gy"), 0, 0, axis_index_groups=groups)


IN_VMEM = pl.BlockSpec(memory_space=pltpu.VMEM)
IN_SMEM = pl.BlockSpec(memory_space=pltpu.SMEM)
IN_HBM = pl.BlockSpec(memory_space=pltpu.HBM)


def one_step(body, in_specs, out_shape, scratch, flops, nbytes, name):
    many = isinstance(out_shape, list)
    return pl.pallas_call(
        body,
        in_specs=in_specs,
        out_specs=[IN_VMEM] * len(out_shape) if many else IN_VMEM,
        out_shape=out_shape,
        scratch_shapes=scratch,
        compiler_params=pltpu.CompilerParams(vmem_limit_bytes=VMEM_LIMIT),
        cost_estimate=pl.CostEstimate(flops=flops, bytes_accessed=nbytes, transcendentals=0),
        name=name,
    )


def one_hot(rows, cols, source):
    row = lax.broadcasted_iota(jnp.int32, (rows, cols), 0)
    col = lax.broadcasted_iota(jnp.int32, (rows, cols), 1)
    return jnp.where(col == source(row), 1.0, 0.0).astype(BF)


def one_hot_rows(rows, cols):
    row = lax.broadcasted_iota(jnp.int32, (rows, cols), 0)
    col = lax.broadcasted_iota(jnp.int32, (rows, cols), 1)
    return jnp.where(col % rows == row, 1.0, 0.0).astype(BF)


def row_statistics_body(tok, out):
    value = tok[...].astype(F32)
    rows = value.shape[0]
    mean = jnp.mean(value, axis=-1, keepdims=True)
    centred = value - mean
    squares = jnp.sum(centred * centred, axis=-1, keepdims=True)
    lane = lax.broadcasted_iota(jnp.int32, (rows, 128), 1)
    cols = jnp.where(lane == 0, mean, jnp.where(lane == 1, squares, 0.0))
    cols = jnp.concatenate([cols, jnp.zeros((128 - rows, 128), F32)], axis=0)
    out[...] = jnp.transpose(cols)[:8]


def row_statistics(tok):
    return one_step(
        row_statistics_body,
        [IN_VMEM],
        jax.ShapeDtypeStruct((8, 128), F32),
        [],
        6 * tok.size,
        tok.size * 2,
        "row_statistics",
    )(tok)


def join(tiles, count):
    mean = sum(t[0:1] for t in tiles) * (1.0 / len(tiles))
    squares = sum(t[1:2] + (t[0:1] - mean) * (t[0:1] - mean) * float(count) for t in tiles)
    return mean, squares


def chip_statistics(mine, other, count):
    def body(a, b, out):
        mean, squares = join([a[...], b[...]], count)
        tile = jnp.concatenate([mean, squares, jnp.zeros((6, 128), F32)], axis=0)
        for k in range(16):
            out[k] = tile

    return one_step(
        body,
        [IN_VMEM] * 2,
        jax.ShapeDtypeStruct((16, 8, 128), F32),
        [],
        16 * 1024,
        18 * 4096,
        "chip_statistics",
    )(mine, other)


def normalise_body(place, b0, b1, b2, b3, tiles, gain, low, high):
    me = jnp.where(place[3] == 0, place[0], place[1])
    count = b0.shape[1]
    order = one_hot(64, 64, lambda o: ((o >> 2) & 1) * 32 + (o >> 3) * 4 + (o & 3))
    for k, block in enumerate((b0, b1, b2, b3)):
        mean, squares = join([tiles[4 * z + ((me + k) & 3)] for z in range(4)], 2 * count)
        inverse = lax.rsqrt(squares * (1.0 / (8 * count)) + 1e-05)
        cols = jnp.transpose(
            jnp.concatenate([mean, inverse, jnp.zeros((126, 128), F32)], axis=0)
        )
        value = block[...].astype(F32)
        value = ((value - cols[:64, 0:1]) * cols[:64, 1:2] * gain[...]).astype(BF)
        value = jnp.dot(order, value, preferred_element_type=F32).astype(BF)
        (low, high)[k // 2][(k % 2) * 64 : (k % 2) * 64 + 64] = value


def normalise(place, blocks, tiles, gain):
    width = blocks[0].shape[1]
    return one_step(
        normalise_body,
        [IN_SMEM] + [IN_VMEM] * 6,
        [jax.ShapeDtypeStruct((128, width), BF)] * 2,
        [],
        256 * width * 6,
        256 * width * 4,
        "normalise",
    )(place, *blocks, tiles, gain)


def project_body(places, place, *refs):
    count = len(places)
    halves = refs[: 2 * count]
    wq, wkv = refs[2 * count : 2 * count + 2]
    far, near = refs[-2:]
    x, y, c = place[0], place[1], place[3]
    nq = wq.shape[1]
    for k, ref in enumerate(halves):
        d1 = places[k // 2]
        q = jnp.dot(ref[...], wq[...], preferred_element_type=F32)
        kv = jnp.dot(ref[...], wkv[...], preferred_element_type=F32)
        for i in range(2):
            d2 = (k % 2) * 2 + i
            bx = (x + jnp.where(c == 0, d2, d1)) & 3
            by = (y + jnp.where(c == 0, d1, d2)) & 3
            slot = by * 2 + (bx & 1)
            rows = slice(i * 64, i * 64 + 64)
            for out, mine in ((near, (bx >> 1) == c), (far, (bx >> 1) != c)):

                @pl.when(mine)
                def _(out=out, slot=slot, rows=rows, q=q, kv=kv):
                    out[slot, :, :nq] = q[rows]
                    out[slot, :, nq:] = kv[rows]


def project(places, place, halves, wq, wkv, held):
    width, nq = wq.shape
    n = nq + wkv.shape[1]
    count = len(places)
    rows = 256 * count
    return pl.pallas_call(
        functools.partial(project_body, places),
        in_specs=[IN_SMEM] + [IN_VMEM] * (2 * count + 2 + len(held)),
        out_specs=[IN_VMEM] * 2,
        out_shape=[jax.ShapeDtypeStruct((8, 64, n), F32)] * 2,
        input_output_aliases={2 * count + 3 + i: i for i in range(len(held))},
        compiler_params=pltpu.CompilerParams(vmem_limit_bytes=VMEM_LIMIT),
        cost_estimate=pl.CostEstimate(
            flops=2 * rows * width * n,
            bytes_accessed=rows * width * 2 + width * n * 2 + rows * n * 4,
            transcendentals=0,
        ),
        name="project",
    )(place, *halves, wq, wkv, *held)


def project_last_body(low, high, wq, wkv, out):
    nq = wq.shape[1]
    for k, ref in enumerate((low, high)):
        q = jnp.dot(ref[...], wq[...], preferred_element_type=F32)
        kv = jnp.dot(ref[...], wkv[...], preferred_element_type=F32)
        out[2 * k : 2 * k + 2, :, :nq] = q.reshape(2, 64, nq)
        out[2 * k : 2 * k + 2, :, nq:] = kv.reshape(2, 64, kv.shape[1])


def project_last(low, high, wq, wkv):
    width, nq = wq.shape
    n = nq + wkv.shape[1]
    return one_step(
        project_last_body,
        [IN_VMEM] * 4,
        jax.ShapeDtypeStruct((4, 64, n), F32),
        [],
        2 * 256 * width * n,
        256 * width * 2 + width * n * 2 + 256 * n * 4,
        "project_last",
    )(low, high, wq, wkv)


def chip_sums_body(place, near, far, late, far_late, out):
    x, y, c = place[0], place[1], place[3]
    for slot in range(8):
        dx = (2 * c + slot % 2 - x) & 3
        dy = (slot // 2 - y) & 3
        mine = jnp.where(jnp.where(c == 0, dy, dx) == 2, late[jnp.where(c == 0, dx, dy)], near[slot])
        other = jnp.where(
            jnp.where(c == 0, dx, dy) == 2, far_late[jnp.where(c == 0, dy, dx)], far[slot]
        )
        out[slot] = (mine + other) * PARTIAL_SCALE


def chip_sums(place, near, far, late, far_late):
    return one_step(
        chip_sums_body,
        [IN_SMEM] + [IN_VMEM] * 4,
        jax.ShapeDtypeStruct(near.shape, F32),
        [],
        2 * near.size,
        near.size * 16,
        "chip_sums",
    )(place, near, far, late, far_late)


def attend_body(lens, x, keys_hbm, values_hbm, out, keys, values, sems):
    nq = out.shape[-1]
    rows, length, dim = keys.shape
    key_copies = [
        pltpu.make_async_copy(keys_hbm.at[row], keys.at[row], sems.at[0, row])
        for row in range(rows)
    ]
    value_copies = [
        pltpu.make_async_copy(values_hbm.at[row], values.at[row], sems.at[1, row])
        for row in range(rows)
    ]
    key_copies[0].start()
    for row in range(rows):
        if row + 1 < rows:
            key_copies[row + 1].start()
        value_copies[row].start()
    piece = 2 * dim // 16
    factor = dim ** (-0.5)
    heads = nq // dim
    flat = x[...].astype(F32).reshape(128, x.shape[-1]).astype(BF)

    lane = lax.broadcasted_iota(jnp.int32, (128, 16 * piece), 1)
    sub = lax.broadcasted_iota(jnp.int32, (128, 16 * piece), 0)
    spread = jnp.where((lane % piece == sub) & (sub < piece), 1.0, 0.0).astype(BF)
    tiled = jnp.dot(flat[:, nq : nq + 128], spread, preferred_element_type=F32)
    tiled = jnp.where(lane // piece == sub >> 3, tiled, 0.0).astype(BF)
    fresh = jnp.dot(one_hot_rows(8, 128), tiled, preferred_element_type=F32)

    count = heads * 32
    step = lax.broadcasted_iota(jnp.int32, (count, 1), 0) & 1
    position = lax.broadcasted_iota(jnp.int32, (1, length), 1)

    def scores_of(row):
        pick = one_hot(32, 128, lambda i: (i >> 1) * 8 + (i & 1) * 4 + row)
        mine = jnp.dot(pick, flat[:, :nq], preferred_element_type=F32).astype(BF)
        query = jnp.concatenate([mine[:, h * dim : (h + 1) * dim] for h in range(heads)], axis=0)
        scores = (
            lax.dot_general(
                query, keys[row], (((1,), (1,)), ((), ())), preferred_element_type=F32
            )
            * factor
        )
        scores = jnp.where(position < lens[row], scores, -1e30)
        query_f = query.astype(F32)
        key_0, key_1 = fresh[row : row + 1, :dim], fresh[rows + row : rows + row + 1, :dim]
        new_0 = jnp.sum(query_f * key_0, axis=-1, keepdims=True) * factor
        new_1 = jnp.sum(query_f * key_1, axis=-1, keepdims=True) * factor
        return scores, new_0, jnp.where(step == 1, new_1, -1e30)

    def weights_of(scores, new_0, new_1):
        top = jnp.maximum(jnp.max(scores, axis=-1, keepdims=True), jnp.maximum(new_0, new_1))
        exp_c = jnp.exp(scores - top)
        exp_0 = jnp.exp(new_0 - top)
        exp_1 = jnp.exp(new_1 - top)
        scale = 1.0 / (jnp.sum(exp_c, axis=-1, keepdims=True) + exp_0 + exp_1)
        return (exp_c * scale).astype(BF), (exp_0 * scale).astype(BF), (exp_1 * scale).astype(BF)

    def mix(row, weight, weight_0, weight_1):
        val_0, val_1 = fresh[row : row + 1, dim:], fresh[rows + row : rows + row + 1, dim:]
        mixed = jnp.dot(weight, values[row], preferred_element_type=F32)
        mixed = mixed + weight_0.astype(F32) * val_0 + weight_1.astype(F32) * val_1
        mixed = mixed.astype(BF)
        mixed = jnp.concatenate([mixed[h * 32 : (h + 1) * 32] for h in range(heads)], axis=1)
        sub = lax.broadcasted_iota(jnp.int32, (128, 32), 0)
        lane = lax.broadcasted_iota(jnp.int32, (128, 32), 1)
        back = jnp.where(sub == (lane >> 1) * 8 + (lane & 1) * 4 + row, 1.0, 0.0).astype(BF)
        return jnp.dot(back, mixed, preferred_element_type=F32)

    key_copies[0].wait()
    ahead = scores_of(0)
    placed = jnp.zeros((128, nq), F32)
    for row in range(rows):
        scores = ahead
        if row + 1 < rows:
            key_copies[row + 1].wait()
        value_copies[row].wait()
        if row + 1 < rows:
            ahead = scores_of(row + 1)
        placed = placed + mix(row, *weights_of(*scores))
    placed = placed.reshape(16, 8, nq).astype(BF)
    for copy in range(4):
        out[copy] = placed


def attend(lens, x, keys, values, nq):
    rows, length, dim = keys.shape
    return pl.pallas_call(
        attend_body,
        in_specs=[IN_SMEM, IN_VMEM, IN_HBM, IN_HBM],
        out_specs=IN_VMEM,
        out_shape=jax.ShapeDtypeStruct((4, 16, 8, nq), BF),
        scratch_shapes=[
            pltpu.VMEM(keys.shape, BF),
            pltpu.VMEM(values.shape, BF),
            pltpu.SemaphoreType.DMA((2, rows)),
        ],
        compiler_params=pltpu.CompilerParams(vmem_limit_bytes=ATTEND_VMEM),
        cost_estimate=pl.CostEstimate(
            flops=4 * rows * 96 * length * dim, bytes_accessed=4 * keys.size, transcendentals=0
        ),
        name="attend",
    )(lens, x, keys, values)


def output_far_body(place, same, cross, w_out, left, half_a, half_b):
    c = place[3]
    depth = left.shape[-1]
    for mixed, bc in ((same, c), (cross, 1 - c)):
        for bz in range(4):
            for half in range(2):
                value = mixed[bz, half * 8 : half * 8 + 8].astype(F32)
                left[bz * 4 + bc * 2 + half] = value.reshape(64, depth).astype(BF)
    partial_rows(place, 2, left, w_out, (half_a, half_b))


def partial_rows(place, d, left, w_out, outs):
    x, y, c = place[0], place[1], place[3]
    group = (jnp.where(c == 0, y, x) + d) & 3
    parts = [left[jnp.where(c == 0, group * 4 + i, i * 4 + group)] for i in range(4)]
    rows = jnp.concatenate(parts, axis=0)
    chunk = w_out.shape[1] // 3
    for j in range(3):
        cols = pl.ds(j * chunk, chunk)
        value = jnp.dot(rows, w_out[:, cols], preferred_element_type=F32).astype(BF)
        at = 0
        for out in outs:
            out[:, cols] = value[at : at + out.shape[0]]
            at += out.shape[0]


def output_far(place, same, cross, w_out):
    depth, width = w_out.shape
    return one_step(
        output_far_body,
        [IN_SMEM] + [IN_VMEM] * 3,
        [jax.ShapeDtypeStruct((16, 64, depth), BF)] + [jax.ShapeDtypeStruct((128, width), BF)] * 2,
        [],
        2 * 256 * depth * width,
        1024 * depth * 4 + depth * width * 2 + 256 * width * 2,
        "output_far",
    )(place, same, cross, w_out)


def output_near_body(place, left, w_out, plus_a, plus_b, minus_a, minus_b):
    partial_rows(place, 1, left, w_out, (plus_a, plus_b))
    partial_rows(place, 3, left, w_out, (minus_a, minus_b))


def output_near(place, left, w_out):
    depth, width = w_out.shape
    return one_step(
        output_near_body,
        [IN_SMEM] + [IN_VMEM] * 2,
        [jax.ShapeDtypeStruct((128, width), BF)] * 4,
        [],
        4 * 256 * depth * width,
        1024 * depth * 2 + depth * width * 2 + 512 * width * 2,
        "output_near",
    )(place, left, w_out)


def output_own_body(place, left, w_out, out):
    partial_rows(place, 0, left, w_out, (out,))


def output_own(place, left, w_out):
    depth, width = w_out.shape
    return one_step(
        output_own_body,
        [IN_SMEM] + [IN_VMEM] * 2,
        jax.ShapeDtypeStruct((256, width), BF),
        [],
        2 * 256 * depth * width,
        1024 * depth * 2 + depth * width * 2 + 256 * width * 2,
        "output_own",
    )(place, left, w_out)


def pair_add_body(a0, a1, b0, b1, a, b):
    a[...] = (a0[...].astype(F32) + a1[...].astype(F32)).astype(BF)
    b[...] = (b0[...].astype(F32) + b1[...].astype(F32)).astype(BF)


def pair_add(a0, a1, b0, b1):
    return one_step(
        pair_add_body,
        [IN_VMEM] * 4,
        [jax.ShapeDtypeStruct(a0.shape, BF)] * 2,
        [],
        2 * a0.size,
        a0.size * 12,
        "pair_add",
    )(a0, a1, b0, b1)


def group_sum_body(place, a, b0, b1, c0, c1, own, s1, s2, s3):
    me = jnp.where(place[3] == 0, place[0], place[1])
    for d, out in enumerate((own, s1, s2, s3)):
        at = (me + d) & 3
        half = pl.ds(pl.multiple_of((at & 1) * 64, 64), 64)
        value = a[pl.ds(pl.multiple_of(at * 64, 64), 64)].astype(F32)
        value = value + jnp.where(at < 2, b0[half], b1[half]).astype(F32)
        value = value + jnp.where(at < 2, c0[half], c1[half]).astype(F32)
        out[...] = value.astype(out.dtype)


def group_sum(place, own, halves):
    width = own.shape[-1]
    return one_step(
        group_sum_body,
        [IN_SMEM] + [IN_VMEM] * 5,
        [jax.ShapeDtypeStruct((64, width), F32)] + [jax.ShapeDtypeStruct((64, width), BF)] * 3,
        [],
        1024 * width,
        1024 * width * 2,
        "group_sum",
    )(place, own, *halves)


def last_sum_body(place, own, r1, r2, r3, out):
    total = own[...] + r1[...].astype(F32) + r2[...].astype(F32) + r3[...].astype(F32)
    order = one_hot(64, 64, lambda o: ((o >> 2) & 7) * 8 + (o >> 5) * 4 + (o & 3))
    total = jnp.dot(order, total.astype(BF), preferred_element_type=F32)
    out[...] = total.reshape(out.shape).astype(BF)


def last_sum(place, own, got):
    rows, width = own.shape
    return one_step(
        last_sum_body,
        [IN_SMEM] + [IN_VMEM] * 4,
        jax.ShapeDtypeStruct((2, rows // 2, width), BF),
        [],
        rows * width * 4,
        rows * width * 12,
        "last_sum",
    )(place, own, *got)


def after(value, other):
    return lax.optimization_barrier((value, other))


def gather_and_project(place, tok, gain, wq, wkv):
    stat = row_statistics(tok)
    b1, b3, b2 = [send(tok, first_axis(d)) for d in (-1, 1, 2)]
    blocks = [tok, b1, b2, b3]
    stat = chip_statistics(stat, send(stat, other_core), tok.shape[1])
    groups = [[2 * z * 16 + 4 * i + j for z in range(4) for j in range(4)] for i in range(4)]
    groups += [
        [(2 * z + 1) * 16 + 4 * j + i for z in range(4) for j in range(4)] for i in range(4)
    ]
    tiles = lax.all_to_all(stat, ("gx", "gy"), 0, 0, axis_index_groups=groups)
    low, high = normalise(place, blocks, tiles, gain)
    minus_low = send(low, second_axis(1))
    plus_high = send(high, second_axis(-1))
    minus_high = send(high, second_axis(1))
    plus_low = send(low, second_axis(-1))
    held = project((0,), place, (low, high), wq, wkv, ())
    near, minus_low = after(held[1], minus_low)
    near, plus_high = after(near, plus_high)
    twice_low = send(minus_low, second_axis(1))
    twice_high = send(plus_high, second_axis(-1))
    held = (held[0], near)
    halves = (plus_low, plus_high, minus_low, minus_high)
    far, near = project((1, 3), place, halves, wq, wkv, held)
    near, twice_low = after(near, twice_low)
    near, twice_high = after(near, twice_high)
    late = project_last(twice_low, twice_high, wq, wkv)
    return chip_sums(place, near, send(far, other_core), late, send(late, other_core))


def per_device(tokens, norm_gain, w_query, w_kv, w_out, cache_keys, cache_values, lengths):
    gx, gy = lax.axis_index("gx"), lax.axis_index("gy")
    z, c, y, x = gx // 2, gx % 2, gy // 4, gy % 4
    width = tokens.shape[2]
    nq = w_query.shape[1]
    piece = w_kv.shape[1] // 16
    place = jnp.stack([x, y, z, c]).astype(jnp.int32)
    gain = norm_gain[None]
    wkv = lax.dynamic_slice_in_dim(w_kv, gy * piece, piece, 1)
    wkv = jnp.pad(wkv, ((0, 0), (0, 128 - piece)))

    partial = gather_and_project(
        place, tokens.reshape(64, width), gain, w_query, wkv
    )
    n = partial.shape[-1]

    partial = exchange(partial.astype(jnp.float16).reshape(64, 8, n))
    query = jnp.sum(partial.astype(F32).reshape(4, 16, 8, n), axis=0) * (1.0 / PARTIAL_SCALE)
    mixed = attend(lengths, query.astype(BF), cache_keys, cache_values, nq)
    mixed = exchange(mixed.reshape(64, 8, nq)).reshape(4, 16, 8, nq)
    cross = send(mixed, other_core)

    left, far_a, far_b = output_far(place, mixed, cross, w_out)
    got_a = send(far_a, second_axis(1))
    got_b = send(far_b, second_axis(-1))
    plus_a, plus_b, minus_a, minus_b = output_near(place, left, w_out)
    from_minus_b = send(plus_b, second_axis(1))
    from_plus_a = send(minus_a, second_axis(-1))
    own = output_own(place, left, w_out)
    plus_a, minus_b = pair_add(plus_a, got_a, minus_b, got_b)
    from_minus_a = send(plus_a, second_axis(1))
    from_plus_b = send(minus_b, second_axis(-1))
    own, s1, s2, s3 = group_sum(
        place, own, [from_minus_a, from_minus_b, from_plus_a, from_plus_b]
    )
    got = [send(s2, first_axis(2)), send(s1, first_axis(1)), send(s3, first_axis(-1))]
    return last_sum(place, own, got)


def solution(mesh):
    in_specs = (
        P(None, "gy", "gx"),
        P("gx"),
        P("gx", "gy"),
        P("gx", None),
        P("gy", "gx"),
        P(("gx", "gy"), None, None),
        P(("gx", "gy"), None, None),
        P(("gx", "gy")),
    )
    out_specs = P(None, "gy", "gx")
    return jax.shard_map(
        per_device, mesh=mesh, in_specs=in_specs, out_specs=out_specs, check_vma=False
    )
```
